256 devices in a mesh: grp: 16 (over y, z_lo), dev: 16 (over z_hi, x, core).
Axes of the slice: x: 4, y: 4, z: 8 (z_hi: 2, z_lo: 4; z = z_hi * 4 + z_lo), core: 2. Of those that a mesh axis runs over, the one named last changes fastest.
Arguments:
- history: bfloat16 [16, 64, 1024], P('grp', 'dev'), may hold values from -6 to 6
- candidates: bfloat16 [16, 16384, 1024], P('grp', 'dev'), may hold values from -6 to 6
- score_grad: float32 [16, 16384], P('grp', 'dev'), may hold values from -0.03125 to 0.03125
- req_counts: int32 [16, 64], P('grp'), may hold values from 1 to 2000, 16384 in all within a row
- owner_slot: int32 [16, 64], P('grp'), may hold values from 0 to 63, each once within a row
- encoder_weight: bfloat16 [1024, 1024], replicated, may hold values from -0.1875 to 0.1875
- user_weight: bfloat16 [1024, 2048], replicated, may hold values from -0.1875 to 0.1875
- cand_weight: bfloat16 [1024, 2048], replicated, may hold values from -0.1875 to 0.1875
- hidden_bias: float32 [2048], replicated, may hold values from -3 to 3
- scorer_weight: float32 [2048], replicated, may hold values from -6 to 6
Outputs:
- cand_gradient: float32 [1024, 2048], P('grp', 'dev')
- user_gradient: float32 [1024, 2048], P('grp', 'dev')
- encoder_gradient: float32 [1024, 1024], P('grp', 'dev')
- scorer_gradient: float32 [2048], replicated
- bias_gradient: float32 [2048], replicated
- history_gradient: float32 [16, 64, 1024], P('grp', 'dev')
The draws below stay inside these ranges and needn't reach their ends.
Inputs may be any that keep to these rules, and one draw needn't show every extreme that they name: `req_counts`: each request has 1 to 2000 candidates, the counts of a group sum to 16384, and one request of each group has exactly 2000. `owner_slot`: each group's map is a permutation: every owner slot holds one request, and slot s lies on the device of index s // 4 along dev.
All inputs are finite; a program needn't handle non-finite values.
Results may differ from the reference program's by a relative error of at most 0.0054.
Values may be sent and summed in bfloat16 or wider, within the bound.
A program may use at most 128 MiB of HBM per device.

```python
import math
import jax
import jax.numpy as jnp
import numpy as np
from jax import lax

D = 1024
H = 2048
C_DEV = 1024
CAND_G = 16384
REQ_G = 64
MOST = 2000
N_GRP = 16
N_DEV = 16


def shard_levels(own_key, dims, shards, smallest, largest):
    gain = 1.0
    for position, blocks in shards:
        steps = jax.random.uniform(jax.random.fold_in(jax.random.fold_in(own_key, 6), position), (blocks,), jnp.float32, smallest / len(shards), largest / len(shards))
        gain = gain * jnp.repeat(jnp.exp(steps), dims[position] // blocks).reshape((-1,) + (1,) * (len(dims) - 1 - position))
    return gain


def profile(amount, total, reach, slope):
    loads = [(1 << 20) // math.isqrt(grade ** slope) + 1 for grade in range(2, amount + 1)]
    surplus, given = total - reach - (amount - 1), [1] * (amount - 1)
    while surplus > 0:
        free = [i for i in range(amount - 1) if given[i] < reach]
        pool, budget = sum([loads[i] for i in free]), surplus
        for i in free:
            extra = min(reach - given[i], max(1, budget * loads[i] // pool), surplus)
            given[i] = given[i] + extra
            surplus = surplus - extra
    return np.array([reach] + given)


def ragged_sizes(rng, number_of, total, limit, skew):
    if number_of == 2:
        one = jax.random.randint(rng, (), max(1, total - limit), min(limit, total - 1) + 1)
        return jnp.stack([one, total - one])
    sizes = jnp.asarray(profile(number_of, total, limit, skew), jnp.int32)
    pairs = (number_of - 1) // 2
    source_of, sink = sizes[1:1 + 2 * pairs:2], sizes[2:2 + 2 * pairs:2]
    slack = jnp.minimum(source_of - 1, limit - sink)
    passed = jax.random.randint(jax.random.fold_in(rng, 1), (pairs,), 0, 1 << 20) % (slack + 1)
    sizes = sizes.at[1:1 + 2 * pairs:2].set(source_of - passed).at[2:2 + 2 * pairs:2].set(sink + passed)
    return sizes[jax.random.permutation(jax.random.fold_in(rng, 2), number_of)]


def scatter_about(rng, extent, spread, reach, pieces=(), kind=jnp.bfloat16):
    factor_of = shard_levels(rng, extent, pieces, -0.22, 0.18) if pieces else 1.0
    entries = jax.random.normal(rng, extent, jnp.float32) * spread * factor_of
    return jnp.minimum(jnp.maximum(entries, -reach), reach).astype(kind)


def setup_inputs(seed: int = 0) -> dict:
    splits = jax.random.split(jax.random.key(seed), 11)
    return {
        "history": scatter_about(splits[0], (N_GRP, REQ_G, D), 1.0, 6.0, ((0, 16), (1, 16))),
        "candidates": scatter_about(splits[1], (N_GRP, CAND_G, D), 1.0, 6.0, ((0, 16), (1, 16))),
        "score_grad": scatter_about(splits[2], (N_GRP, CAND_G), ((C_DEV * N_DEV * N_GRP) ** -0.5), 0.03125, ((0, 16), (1, 16)), jnp.float32),
        "req_counts": jax.vmap(lambda own: ragged_sizes(own, REQ_G, CAND_G, MOST, 2))(jax.random.split(splits[3], N_GRP)).reshape((N_GRP, REQ_G)).astype(jnp.int32),
        "owner_slot": jax.vmap(lambda own: jax.random.permutation(own, REQ_G))(jax.random.split(splits[4], N_GRP)).reshape((N_GRP, REQ_G)).astype(jnp.int32),
        "encoder_weight": scatter_about(splits[5], (D, D), D ** -0.5, 0.1875),
        "user_weight": scatter_about(splits[6], (D, H), D ** -0.5, 0.1875),
        "cand_weight": scatter_about(splits[7], (D, H), D ** -0.5, 0.1875),
        "hidden_bias": scatter_about(splits[8], (H,), 0.5, 3.0, (), jnp.float32),
        "scorer_weight": scatter_about(splits[9], (H,), 1.0, 6.0, (), jnp.float32),
    }


def silu_parts(values):
    sigma = jax.nn.sigmoid(values)
    return values * sigma, sigma * (1.0 + values * (1.0 - sigma))


def reference(history, candidates, score_grad, req_counts, owner_slot, encoder_weight, user_weight, cand_weight, hidden_bias, scorer_weight):
    highest = lax.Precision.HIGHEST

    def one_group(totals, group_data):
        history_rows, cand_rows, dscore, counts_group, slot_map = group_data
        enc_pre = jnp.dot(history_rows, encoder_weight, preferred_element_type=jnp.float32)
        enc_act, enc_slope = silu_parts(enc_pre)
        user_vec = (history_rows.astype(jnp.float32) + enc_act).astype(jnp.bfloat16)
        user_proj = jnp.dot(user_vec, user_weight, preferred_element_type=jnp.float32).astype(jnp.bfloat16)
        req_ends = jnp.cumsum(counts_group).astype(jnp.int32)
        row_index = jnp.arange(CAND_G, dtype=jnp.int32)
        request_id = jnp.sum((req_ends[None, :] <= row_index[:, None]).astype(jnp.int32), axis=1).astype(jnp.int32)
        slot_id = slot_map[request_id].astype(jnp.int32)
        pre_act = jnp.dot(cand_rows, cand_weight, preferred_element_type=jnp.float32) + user_proj[slot_id].astype(jnp.float32) + hidden_bias[None, :]
        hidden_act, hidden_slope = silu_parts(pre_act)
        pre_grad = dscore[:, None] * scorer_weight[None, :] * hidden_slope
        grad_half = pre_grad.astype(jnp.bfloat16)
        cand_term = jnp.dot(cand_rows.T, grad_half, preferred_element_type=jnp.float32)
        scorer_term = jnp.sum(dscore[:, None] * hidden_act, axis=0)
        bias_term = jnp.sum(pre_grad, axis=0)
        slot_grad = jax.ops.segment_sum(grad_half.astype(jnp.float32), slot_id, num_segments=REQ_G)
        user_term = jnp.dot(user_vec.astype(jnp.float32).T, slot_grad, precision=highest)
        user_grad = jnp.dot(slot_grad.astype(jnp.bfloat16), user_weight.T, preferred_element_type=jnp.float32)
        enc_grad = (user_grad * enc_slope).astype(jnp.bfloat16)
        enc_term = jnp.dot(history_rows.T, enc_grad, preferred_element_type=jnp.float32)
        history_grad = user_grad + jnp.dot(enc_grad, encoder_weight.T, preferred_element_type=jnp.float32)
        summed = (totals[0] + cand_term, totals[1] + user_term, totals[2] + enc_term, totals[3] + scorer_term, totals[4] + bias_term)
        return summed, history_grad

    zeros_init = (jnp.zeros((D, H), jnp.float32), jnp.zeros((D, H), jnp.float32), jnp.zeros((D, D), jnp.float32), jnp.zeros((H,), jnp.float32), jnp.zeros((H,), jnp.float32))
    totals, history_gradient = lax.scan(one_group, zeros_init, (history, candidates, score_grad, req_counts, owner_slot))
    return (totals[0], totals[1], totals[2], totals[3], totals[4], history_gradient)
```

```python
import jax
import jax.numpy as jnp
from jax import lax
from jax.experimental import pallas as pl
from jax.experimental.pallas import tpu as pltpu
from jax.sharding import PartitionSpec as P

f32 = jnp.float32
bf16 = jnp.bfloat16
MESH = pl.DeviceIdType.MESH

D = 1024
H = 2048
C = 1024
SLOTS = 64
KAUG = D + 128
ROWS = D + SLOTS
CHUNK = 256


def ds(start, size):
    return pl.ds(pl.multiple_of(start, size), size)


def split(value):
    high = value.astype(bf16).astype(f32)
    return high, value - high


def kernel(
    hist_ref,
    dscore_ref,
    counts_ref,
    slot_ref,
    bias_ref,
    scorer_ref,
    cand_hbm,
    we_hbm,
    wu_hbm,
    wc_hbm,
    cg_ref,
    ug_ref,
    eg_ref,
    sc_ref,
    bi_ref,
    hg_ref,
    xs,
    xt,
    we,
    wu,
    wcs,
    dcol,
    z,
    hp32,
    hgat,
    hgat32,
    h32,
    uh,
    eslope,
    grx,
    part,
    csend,
    crecv,
    s32,
    asend,
    arecv,
    aown,
    bsend,
    brecv,
    bown,
    ssend,
    srecv,
    sown,
    msg,
    sgf,
    mrecv,
    a2send,
    a2recv,
    b2send,
    b2recv,
    tt32,
    zsend,
    zrecv,
    ug32,
    enc,
    erecv,
    fsend,
    frecv,
    ld,
    h_s,
    h_r,
    g_s,
    g_r,
    c_s,
    c_r,
    a_s,
    a_r,
    b_s,
    b_r,
    s_s,
    s_r,
    md_s,
    md_r,
    mg_s,
    mg_r,
    a2_s,
    a2_r,
    b2_s,
    b2_r,
    z_s,
    z_r,
    e_s,
    e_r,
    f_s,
    f_r,
):
    g = lax.axis_index("grp")
    d = lax.axis_index("dev")
    y, zl = lax.div(g, 4), lax.rem(g, 4)
    zh, x, c = lax.div(d, 8), lax.rem(lax.div(d, 2), 4), lax.rem(d, 2)

    def dev_of(zh_, x_):
        return zh_ * 8 + x_ * 2 + c

    def block_of(k):
        zh_ = lax.rem(zh + 1 + lax.div(k, 4), 2)
        x_ = lax.rem(x + 1 + lax.rem(k, 4), 4)
        return zh_, x_

    def remote(src, dst, send, recv, to):
        return pltpu.make_async_remote_copy(
            src_ref=src,
            dst_ref=dst,
            send_sem=send,
            recv_sem=recv,
            device_id=to,
            device_id_type=MESH,
        )

    loads = [
        pltpu.make_async_copy(we_hbm, we, ld.at[0]),
        pltpu.make_async_copy(cand_hbm.at[0], xs.at[:, pl.ds(0, D)], ld.at[1]),
        pltpu.make_async_copy(wu_hbm, wu, ld.at[2]),
        pltpu.make_async_copy(wc_hbm, wcs.at[pl.ds(0, D)], ld.at[3]),
    ]
    for load in loads:
        load.start()

    barrier = pltpu.get_barrier_semaphore()

    @pl.loop(1, 16)
    def _(j):
        pl.semaphore_signal(
            barrier, inc=1, device_id=(g, lax.rem(d + j, 16)), device_id_type=MESH
        )
        pl.semaphore_signal(
            barrier, inc=1, device_id=(lax.rem(g + j, 16), d), device_id_type=MESH
        )

    @pl.loop(1, 4)
    def _(j):
        pl.semaphore_signal(
            barrier,
            inc=1,
            device_id=(y * 4 + lax.rem(zl + j, 4), dev_of(1 - zh, x)),
            device_id_type=MESH,
        )

    hist = hist_ref[0].astype(f32)
    for k in range(8):
        hp32[pl.ds(4 * k, 4), :] = hist[:, 128 * k : 128 * k + 128]
    hgat[d] = hp32[...].astype(bf16)
    pl.semaphore_wait(barrier, 33)

    def hist_copy(j):
        return remote(
            hgat.at[d], hgat.at[d], h_s.at[j], h_r.at[j], (g, lax.rem(d + j, 16))
        )

    @pl.loop(1, 16)
    def _(j):
        hist_copy(j).start()

    r_i = lax.broadcasted_iota(jnp.int32, (SLOTS, SLOTS), 0)
    c_i = lax.broadcasted_iota(jnp.int32, (SLOTS, SLOTS), 1)
    counts = jnp.broadcast_to(counts_ref[...], (SLOTS, SLOTS)).astype(f32)
    slots = jnp.broadcast_to(slot_ref[...], (SLOTS, SLOTS)).astype(f32)
    ends = jnp.sum(jnp.where(c_i <= r_i, counts, 0.0), axis=1, keepdims=True)
    starts = jnp.sum(jnp.where(c_i < r_i, counts, 0.0), axis=1, keepdims=True)
    mine = jnp.sum(jnp.where(c_i == r_i, slots, 0.0), axis=1, keepdims=True)
    r_w = lax.broadcasted_iota(jnp.int32, (SLOTS, 128), 1).astype(f32)
    hit = r_w == mine
    start_row = jnp.sum(jnp.where(hit, starts, 0.0), axis=0, keepdims=True)
    end_row = jnp.sum(jnp.where(hit, ends, 0.0), axis=0, keepdims=True)
    base = (d * C).astype(f32)
    lane = lax.broadcasted_iota(jnp.int32, (CHUNK, 128), 1)
    ones = jnp.where((lane >= SLOTS) & (lane < SLOTS + 3), 1.0, 0.0)
    for r in range(C // CHUNK):
        row = lax.broadcasted_iota(jnp.int32, (CHUNK, 128), 0).astype(f32) + (base + r * CHUNK)
        sel = jnp.where((row >= start_row) & (row < end_row), 1.0, 0.0)
        xs[pl.ds(r * CHUNK, CHUNK), pl.ds(D, 128)] = (sel + ones).astype(bf16)
        for q in range(CHUNK // 128):
            xt[pl.ds(D, SLOTS), pl.ds(r * CHUNK + q * 128, 128)] = (
                sel[q * 128 : q * 128 + 128].T[:SLOTS].astype(bf16)
            )
    for r in range(8):
        dcol[pl.ds(r * 128, 128), :] = jnp.broadcast_to(dscore_ref[r : r + 1, :], (128, 128)).T
    loads[1].wait()
    for r in range(4):
        for q in range(4):
            xt[pl.ds(q * 256, 256), pl.ds(r * 256, 256)] = xs[
                pl.ds(r * 256, 256), pl.ds(q * 256, 256)
            ].T

    @pl.loop(1, 16)
    def _(j):
        hist_copy(j).wait_recv()

    hgat32[...] = hgat[...].astype(f32).reshape(512, 128)
    for i in range(16):
        for k in range(8):
            h32[pl.ds(4 * i, 4), pl.ds(128 * k, 128)] = hgat32[pl.ds(32 * i + 4 * k, 4), :]
    uh[pl.ds(64, 64), :] = h32[...].astype(bf16)
    loads[0].wait()
    pre = jnp.dot(uh[pl.ds(64, 64), :], we[...], preferred_element_type=f32)
    sig = 0.5 * jnp.tanh(0.5 * pre) + 0.5
    act = pre * sig
    eslope[...] = sig + act * (1.0 - sig)
    uh[pl.ds(0, 64), :] = (h32[...] + act).astype(bf16)

    def group_copy(j):
        g_to = lax.rem(g + j, 16)
        return remote(
            uh.at[:, ds(lax.div(g_to, 2) * 128, 128)],
            grx.at[g],
            g_s.at[j],
            g_r.at[j],
            (g_to, d),
        )

    @pl.loop(1, 16)
    def _(j):
        group_copy(j).start()

    grx[g] = uh[:, ds(lax.div(g, 2) * 128, 128)]
    loads[2].wait()
    loads[3].wait()

    def core_copy(k):
        return remote(csend.at[k], crecv.at[k], c_s.at[k], c_r.at[k], (g, d + 1 - 2 * c))

    def a_copy(k):
        _, x_ = block_of(k)
        return remote(asend.at[k], arecv.at[k], a_s.at[k], a_r.at[k], (g, dev_of(zh, x_)))

    def b_copy(k, j):
        y_ = lax.rem(y + j, 4)
        return remote(
            bsend.at[k, y_], brecv.at[k, j], b_s.at[k * 4 + j], b_r.at[k * 4 + j], (y_ * 4 + zl, d)
        )

    def s_copy(k):
        return remote(ssend.at[k], srecv.at[k], s_s.at[k], s_r.at[k], (g, dev_of(*block_of(k))))

    def both(ref, n, rows=slice(None)):
        first = ref[rows, ds(n * 256 + c * 128, 128)]
        second = ref[rows, ds(n * 256 + (1 - c) * 128, 128)]
        return jnp.concatenate([first, second], axis=1)

    def compute(k):
        zh_, x_ = block_of(k)
        n = zh_ * 4 + x_
        proj = jnp.dot(uh[pl.ds(0, 64), :], both(wu, n), preferred_element_type=f32).astype(bf16)
        bias = both(bias_ref, n)
        b0, rest = split(bias)
        b1, b2 = split(rest)
        line = lax.broadcasted_iota(jnp.int32, (64, 256), 0)
        tail = jnp.where(line == 0, b0, jnp.where(line == 1, b1, jnp.where(line == 2, b2, 0.0)))
        weights = jnp.concatenate(
            [both(wcs, n, pl.ds(0, D)), proj, tail.astype(bf16)], axis=0
        )
        scorer = both(scorer_ref, n)
        total = jnp.zeros((8, 256), f32)
        for r in range(C // CHUNK):
            rows = pl.ds(r * CHUNK, CHUNK)
            v = jnp.dot(xs[rows, :], weights, preferred_element_type=f32)
            sigma = 0.5 * jnp.tanh(0.5 * v) + 0.5
            hidden = v * sigma
            slope = sigma + hidden * (1.0 - sigma)
            score = dcol[rows, :]
            score = jnp.concatenate([score, score], axis=1)
            z[rows, :] = (score * scorer * slope).astype(bf16)
            total = total + jnp.sum((score * hidden).reshape(CHUNK // 8, 8, 256), axis=0)
        term = jnp.dot(xt[...], z[...], preferred_element_type=f32)
        part[lax.rem(k, 2), pl.ds(0, ROWS), :] = term[:, :128]
        csend[k, pl.ds(0, ROWS), :] = term[:, 128:].astype(bf16)
        s_hi, s_lo = split(jnp.sum(total, axis=0, keepdims=True))
        line = lax.broadcasted_iota(jnp.int32, (16, 256), 0)
        aux = jnp.where(line == 0, s_hi, jnp.where(line == 1, s_lo, 0.0))
        part[lax.rem(k, 2), pl.ds(ROWS, 16), :] = aux[:, :128]
        csend[k, pl.ds(ROWS, 16), :] = aux[:, 128:].astype(bf16)
        core_copy(k).start()

    def stage(k):
        core_copy(k).wait_recv()
        total = part[lax.rem(k, 2)] + crecv[k].astype(f32)
        s32[...] = total
        half = total.astype(bf16)
        for y_ in range(4):
            asend[k, pl.ds(y_ * 128, 128), :] = half[y_ * 256 : y_ * 256 + 128]
            bsend[k, y_] = half[y_ * 256 + 128 : y_ * 256 + 256]

        @pl.loop(1, 4)
        def _(j):
            b_copy(k, j).start()

        @pl.when(lax.rem(k, 4) != 3)
        def _():
            a_copy(k).start()

        @pl.when(lax.rem(k, 4) == 3)
        def _():
            for y_ in range(4):
                aown[lax.div(k, 4), pl.ds(y_ * 128, 128), :] = s32[pl.ds(y_ * 256, 128), :]

        line = lax.broadcasted_iota(jnp.int32, (16, 128), 0)
        aux = total[ROWS:]
        t_hi, t_lo = split(aux[0:1] + aux[1:2])
        tail = jnp.where(line == 0, t_hi, jnp.where(line == 1, t_lo, 0.0))

        @pl.when(k != 7)
        def _():
            ssend[k, pl.ds(0, SLOTS), :] = half[D:ROWS]
            ssend[k, pl.ds(SLOTS, 16), :] = tail.astype(bf16)
            s_copy(k).start()

        @pl.when(k == 7)
        def _():
            sown[pl.ds(0, SLOTS), :] = total[D:ROWS]
            sown[pl.ds(SLOTS, 16), :] = tail

        bown[k] = s32[pl.ds(pl.multiple_of(y * 256 + 128, 128), 128), :]

    @pl.loop(0, 8)
    def _(k):
        compute(k)

        @pl.when(k > 0)
        def _():
            stage(k - 1)

    stage(7)

    slot_sum = sown[...]
    for k in range(7):
        s_copy(k).wait_recv()
        slot_sum = slot_sum + srecv[k].astype(f32)
    rows64 = slot_sum[:SLOTS]
    b_hi, b_lo = split(jnp.sum(rows64, axis=0, keepdims=True))
    q_hi, q_lo = split(slot_sum[SLOTS : SLOTS + 1] + slot_sum[SLOTS + 1 : SLOTS + 2])
    line = lax.broadcasted_iota(jnp.int32, (16, 128), 0)
    tail = jnp.where(
        line == 0,
        b_hi,
        jnp.where(line == 1, b_lo, jnp.where(line == 2, q_hi, jnp.where(line == 3, q_lo, 0.0))),
    )
    msg[pl.ds(0, SLOTS), :] = rows64.astype(bf16)
    msg[pl.ds(SLOTS, 16), :] = tail.astype(bf16)

    def dev_msg(j):
        return remote(
            msg.at[pl.ds(0, SLOTS)],
            sgf.at[:, ds(d * 128, 128)],
            md_s.at[j],
            md_r.at[j],
            (g, lax.rem(d + j, 16)),
        )

    def grp_msg(j):
        return remote(msg, mrecv.at[g], mg_s.at[j], mg_r.at[j], (lax.rem(g + j, 16), d))

    @pl.loop(1, 16)
    def _(j):
        dev_msg(j).start()

    sgf[:, ds(d * 128, 128)] = msg[pl.ds(0, SLOTS), :]
    mrecv[g] = msg[...]

    def a2_copy(j):
        y_ = lax.rem(y + j, 4)
        return remote(a2send.at[y_], a2recv.at[j], a2_s.at[j], a2_r.at[j], (y_ * 4 + zl, d))

    def b2_copy(k):
        _, x_ = block_of(k)
        return remote(b2send.at[k], b2recv.at[k], b2_s.at[k], b2_r.at[k], (g, dev_of(zh, x_)))

    for kk in range(2):
        total = aown[kk]
        for j in range(3):
            a_copy(4 * kk + j).wait_recv()
            total = total + arecv[4 * kk + j].astype(f32)
        aown[kk] = total
        half = total.astype(bf16)
        for y_ in range(4):
            a2send[y_, kk] = half[y_ * 128 : y_ * 128 + 128]

    @pl.loop(1, 4)
    def _(j):
        a2_copy(j).start()

    @pl.loop(0, 8)
    def _(k):
        total = bown[k]
        for j in range(1, 4):
            b_copy(k, j).wait_recv()
            total = total + brecv[k, j].astype(f32)
        bown[k] = total
        b2send[k] = total.astype(bf16)

        @pl.when(lax.rem(k, 4) != 3)
        def _():
            b2_copy(k).start()

    @pl.loop(1, 16)
    def _(j):
        grp_msg(j).start()

    @pl.loop(1, 16)
    def _(j):
        dev_msg(j).wait_recv()

    user_grad = lax.dot_general(
        sgf[...], wu[...], (((1,), (1,)), ((), ())), preferred_element_type=f32
    )
    ug32[...] = user_grad
    enc[...] = (user_grad * eslope[...]).astype(bf16)

    def enc_copy(j):
        return remote(
            enc.at[:, ds(lax.div(d, 2) * 128, 128)],
            erecv.at[g],
            e_s.at[j],
            e_r.at[j],
            (lax.rem(g + j, 16), d),
        )

    @pl.loop(1, 16)
    def _(j):
        enc_copy(j).start()

    erecv[g] = enc[:, ds(lax.div(d, 2) * 128, 128)]

    @pl.loop(1, 4)
    def _(j):
        a2_copy(j).wait_recv()

    for kk in range(2):
        ta = aown[kk, pl.ds(pl.multiple_of(y * 128, 128), 128), :]
        for j in range(1, 4):
            ta = ta + a2recv[j, kk].astype(f32)
        tb = bown[4 * kk + 3]
        for j in range(3):
            b2_copy(4 * kk + j).wait_recv()
            tb = tb + b2recv[4 * kk + j].astype(f32)
        for zl_, piece in enumerate((ta[:64], ta[64:], tb[:64], tb[64:])):
            tt32[kk, zl_] = piece
            zsend[kk, zl_] = piece.astype(bf16)

    def z_copy(kk, j):
        zl_ = lax.rem(zl + j, 4)
        zh_ = lax.rem(zh + 1 + kk, 2)
        return remote(
            zsend.at[kk, zl_],
            zrecv.at[kk, j],
            z_s.at[kk * 4 + j],
            z_r.at[kk * 4 + j],
            (y * 4 + zl_, dev_of(zh_, x)),
        )

    for kk, j in [(0, 0), (0, 1), (0, 2), (0, 3), (1, 1), (1, 2), (1, 3)]:
        z_copy(kk, j).start()

    eight = ds(lax.div(d, 2) * 8, 8)
    ug_rows = ug32[eight, :]
    enc_rows = (ug_rows * eslope[eight, :]).astype(bf16)
    hist_grad = ug_rows + lax.dot_general(
        enc_rows, we[...], (((1,), (1,)), ((), ())), preferred_element_type=f32
    )
    hg_ref[0] = jnp.where(c == 0, hist_grad[:4], hist_grad[4:])

    @pl.loop(1, 16)
    def _(j):
        group_copy(j).wait_recv()
        grp_msg(j).wait_recv()

    user_cols = grx[:, pl.ds(0, 64), :].reshape(1024, 128)
    hist_cols = grx[:, pl.ds(64, 64), :].reshape(1024, 128)
    slot_cols = mrecv[:, pl.ds(0, 64), :].reshape(1024, 128)
    user_out = jnp.dot(user_cols.T, slot_cols, preferred_element_type=f32)
    odd = lax.rem(g, 2)
    ug_ref[...] = jnp.where(odd == 0, user_out[:64], user_out[64:])
    tails = jnp.sum(mrecv[:, pl.ds(64, 16), :].astype(f32), axis=0)
    line = lax.broadcasted_iota(jnp.int32, (8, 128), 0)
    fsend[...] = jnp.where(
        line == 0, tails[0:1] + tails[1:2], jnp.where(line == 1, tails[2:3] + tails[3:4], 0.0)
    )

    def f_copy(j):
        return remote(fsend, frecv.at[d], f_s.at[j], f_r.at[j], (g, lax.rem(d + j, 16)))

    @pl.loop(1, 16)
    def _(j):
        f_copy(j).start()

    frecv[d] = fsend[...]

    @pl.loop(1, 16)
    def _(j):
        enc_copy(j).wait_recv()

    enc_out = jnp.dot(hist_cols.T, erecv[...].reshape(1024, 128), preferred_element_type=f32)
    enc_out = jnp.where(odd == 0, enc_out[:64], enc_out[64:])
    eg_ref[...] = jnp.where(c == 0, enc_out[:, :64], enc_out[:, 64:])

    cand = tt32[1, zl]
    for kk, j in [(0, 0), (0, 1), (0, 2), (0, 3), (1, 1), (1, 2), (1, 3)]:
        z_copy(kk, j).wait_recv()
        cand = cand + zrecv[kk, j].astype(f32)
    cg_ref[...] = cand

    @pl.loop(1, 16)
    def _(j):
        f_copy(j).wait_recv()

    final = frecv[...]
    bi_ref[...] = final[:, 0, :]
    sc_ref[...] = final[:, 1, :]

    @pl.loop(1, 16)
    def _(j):
        hist_copy(j).wait_send()
        group_copy(j).wait_send()
        dev_msg(j).wait_send()
        grp_msg(j).wait_send()
        enc_copy(j).wait_send()
        f_copy(j).wait_send()

    @pl.loop(0, 8)
    def _(k):
        core_copy(k).wait_send()
        for j in range(1, 4):
            b_copy(k, j).wait_send()

        @pl.when(lax.rem(k, 4) != 3)
        def _():
            a_copy(k).wait_send()
            b2_copy(k).wait_send()

        @pl.when(k != 7)
        def _():
            s_copy(k).wait_send()

    @pl.loop(1, 4)
    def _(j):
        a2_copy(j).wait_send()

    for kk, j in [(0, 0), (0, 1), (0, 2), (0, 3), (1, 1), (1, 2), (1, 3)]:
        z_copy(kk, j).wait_send()


def local(
    history,
    candidates,
    score_grad,
    req_counts,
    owner_slot,
    encoder_weight,
    user_weight,
    cand_weight,
    hidden_bias,
    scorer_weight,
):
    vmem = pl.BlockSpec(memory_space=pltpu.VMEM)
    hbm = pl.BlockSpec(memory_space=pl.ANY)
    V = pltpu.VMEM
    dma = lambda n: pltpu.SemaphoreType.DMA((n,))
    scratch = [
        V((C, KAUG), bf16),
        V((ROWS, C), bf16),
        V((D, D), bf16),
        V((D, H), bf16),
        V((D, H), bf16),
        V((C, 128), f32),
        V((C, 256), bf16),
        V((32, 128), f32),
        V((16, 32, 128), bf16),
        V((512, 128), f32),
        V((64, D), f32),
        V((128, D), bf16),
        V((64, D), f32),
        V((16, 128, 128), bf16),
        V((2, ROWS + 16, 128), f32),
        V((8, ROWS + 16, 128), bf16),
        V((8, ROWS + 16, 128), bf16),
        V((ROWS + 16, 128), f32),
        V((8, 512, 128), bf16),
        V((8, 512, 128), bf16),
        V((2, 512, 128), f32),
        V((8, 4, 128, 128), bf16),
        V((8, 4, 128, 128), bf16),
        V((8, 128, 128), f32),
        V((8, 80, 128), bf16),
        V((8, 80, 128), bf16),
        V((80, 128), f32),
        V((80, 128), bf16),
        V((64, H), bf16),
        V((16, 80, 128), bf16),
        V((4, 2, 128, 128), bf16),
        V((4, 2, 128, 128), bf16),
        V((8, 128, 128), bf16),
        V((8, 128, 128), bf16),
        V((2, 4, 64, 128), f32),
        V((2, 4, 64, 128), bf16),
        V((2, 4, 64, 128), bf16),
        V((64, D), f32),
        V((64, D), bf16),
        V((16, 64, 128), bf16),
        V((8, 128), f32),
        V((16, 8, 128), f32),
        dma(4),
    ]
    for n in (16, 16, 8, 8, 32, 8, 16, 16, 4, 8, 8, 16, 16):
        scratch += [dma(n), dma(n)]
    outs = pl.pallas_call(
        kernel,
        out_shape=(
            jax.ShapeDtypeStruct((64, 128), f32),
            jax.ShapeDtypeStruct((64, 128), f32),
            jax.ShapeDtypeStruct((64, 64), f32),
            jax.ShapeDtypeStruct((16, 128), f32),
            jax.ShapeDtypeStruct((16, 128), f32),
            jax.ShapeDtypeStruct((1, 4, D), f32),
        ),
        in_specs=[vmem] * 6 + [hbm] * 4,
        out_specs=(vmem,) * 6,
        scratch_shapes=scratch,
        compiler_params=pltpu.CompilerParams(
            collective_id=0, has_side_effects=True, vmem_limit_bytes=56 * 2**20
        ),
        name="ranking_backward",
    )(
        history,
        score_grad.reshape(8, 128),
        req_counts,
        owner_slot,
        hidden_bias.reshape(1, H),
        scorer_weight.reshape(1, H),
        candidates,
        encoder_weight,
        user_weight,
        cand_weight,
    )
    cg, ug, eg, sc, bi, hg = outs
    return (cg, ug, eg, sc.reshape(H), bi.reshape(H), hg)


def solution(mesh):
    in_specs = (
        P("grp", "dev", None),
        P("grp", "dev", None),
        P("grp", "dev"),
        P("grp", None),
        P("grp", None),
        P(),
        P(),
        P(),
        P(),
        P(),
    )
    out_specs = (P("grp", "dev"), P("grp", "dev"), P("grp", "dev"), P(), P(), P("grp", "dev", None))
    return jax.shard_map(local, mesh=mesh, in_specs=in_specs, out_specs=out_specs, check_vma=False)
```

```python
import jax
import jax.numpy as jnp
from jax import lax
from jax.experimental import pallas as pl
from jax.experimental.pallas import tpu as pltpu
from jax.sharding import PartitionSpec as P

f32 = jnp.float32
bf16 = jnp.bfloat16
MESH = pl.DeviceIdType.MESH

D = 1024
H = 2048
C = 1024
SLOTS = 64
ROWS = D + SLOTS
HALF = 512
PACKED = 288
CHUNK = 256


def ds(start, size):
    return pl.ds(pl.multiple_of(start, size), size)


def split(value):
    high = value.astype(bf16).astype(f32)
    return high, value - high


def kernel(
    hist_ref,
    dscore_ref,
    counts_ref,
    slot_ref,
    bias_ref,
    scorer_ref,
    cand_hbm,
    we_hbm,
    wu_hbm,
    wc_hbm,
    out_ref,
    xs,
    sel_s,
    xt,
    we,
    wu,
    wc,
    dcol,
    ahead,
    z0,
    z1,
    picked0,
    picked1,
    acts,
    hp32,
    hgat,
    hgat32,
    h32,
    uh,
    eslope,
    grx,
    part,
    csend,
    crecv,
    s32,
    lsend,
    lrecv,
    lown,
    asend,
    arecv,
    aown,
    bsend,
    brecv,
    bown,
    ssend,
    srecv,
    msg,
    sgf,
    mrecv,
    a2send,
    a2recv,
    b2send,
    b2recv,
    tt32,
    zsend,
    zrecv,
    ug32,
    enc,
    erecv,
    u32,
    usend,
    urecv,
    n32,
    nsend,
    nrecv,
    tsend,
    trecv,
    frecv,
    ld,
    h_s,
    h_r,
    g_s,
    g_r,
    c_s,
    c_r,
    a_s,
    a_r,
    b_s,
    b_r,
    l_s,
    l_r,
    s_s,
    s_r,
    md_s,
    md_r,
    my_s,
    my_r,
    a2_s,
    a2_r,
    b2_s,
    b2_r,
    z_s,
    z_r,
    e_s,
    e_r,
    u_s,
    u_r,
    n_s,
    n_r,
    t_s,
    t_r,
    f_s,
    f_r,
):
    g = lax.axis_index("grp")
    d = lax.axis_index("dev")
    y, zl = lax.div(g, 4), lax.rem(g, 4)
    zh, x, c = lax.div(d, 8), lax.rem(lax.div(d, 2), 4), lax.rem(d, 2)
    chip = lax.div(d, 2)
    other = d + 1 - 2 * c
    far = lax.rem(d + 8, 16)

    def dev_of(zh_, x_):
        return zh_ * 8 + x_ * 2 + c

    def chip_peer(j):
        return (g, lax.rem(chip + j, 8) * 2 + c)

    def y_peer(j):
        return (lax.rem(y + j, 4) * 4 + zl, d)

    def z_peer(kk, j):
        return (y * 4 + lax.rem(zl + j, 4), dev_of(lax.rem(zh + 1 + kk, 2), x))

    def block_of(k):
        zh_ = lax.rem(zh + 1 + lax.div(k, 4), 2)
        i = lax.rem(k, 4)
        x_ = lax.rem(x + 2 + 3 * i + 3 * lax.div(i * (i - 1), 2), 4)
        return zh_, x_

    def remote(src, dst, send, recv, to):
        return pltpu.make_async_remote_copy(
            src_ref=src,
            dst_ref=dst,
            send_sem=send,
            recv_sem=recv,
            device_id=to,
            device_id_type=MESH,
        )

    def gather(ref_of, send, recv):
        def own(j):
            return remote(ref_of(d), ref_of(d), send.at[j], recv.at[j], chip_peer(j))

        def beside():
            return remote(ref_of(d), ref_of(d), send.at[0], recv.at[0], (g, other))

        def onward(j):
            i = lax.rem(chip + 8 - j, 8) * 2 + c
            return remote(ref_of(i), ref_of(i), send.at[8 + j], recv.at[8 + j], (g, other))

        def start():
            @pl.loop(1, 8)
            def _(j):
                own(j).start()

            beside().start()

        def forward_all():
            @pl.loop(1, 8)
            def _(j):
                own(j).wait_recv()
                onward(j).start()

        def finish_recv():
            beside().wait_recv()

            @pl.loop(1, 8)
            def _(j):
                onward(j).wait_recv()

        def finish_send():
            beside().wait_send()

            @pl.loop(1, 8)
            def _(j):
                own(j).wait_send()
                onward(j).wait_send()

        return start, forward_all, finish_recv, finish_send

    loads = [
        pltpu.make_async_copy(cand_hbm.at[0], xs, ld.at[0]),
        pltpu.make_async_copy(wc_hbm, wc, ld.at[1]),
        pltpu.make_async_copy(we_hbm, we, ld.at[2]),
        pltpu.make_async_copy(wu_hbm, wu, ld.at[3]),
    ]
    for load in loads:
        load.start()

    barrier = pltpu.get_barrier_semaphore()

    def greet(to):
        pl.semaphore_signal(barrier, inc=1, device_id=to, device_id_type=MESH)

    greet((g, other))

    @pl.loop(1, 4)
    def _(j):
        greet(z_peer(0, j))
        greet(z_peer(1, j))
        greet(y_peer(j))

    @pl.loop(1, 8)
    def _(j):
        greet(chip_peer(j))

    hist = hist_ref[0].astype(f32)
    for k in range(8):
        hp32[pl.ds(4 * k, 4), :] = hist[:, 128 * k : 128 * k + 128]
    hgat[d] = hp32[...].astype(bf16)
    hist_start, hist_forward, hist_recv, hist_send = gather(lambda i: hgat.at[i], h_s, h_r)

    def both(ref, n, rows=slice(None)):
        first = ref[rows, ds(n * 256 + c * 128, 128)]
        second = ref[rows, ds(n * 256 + (1 - c) * 128, 128)]
        return jnp.concatenate([first, second], axis=1)

    def number(k):
        zh_, x_ = block_of(k)
        return zh_ * 4 + x_

    def forward(k):
        ahead[k] = jnp.dot(xs[...], both(wc, number(k)), preferred_element_type=f32)

    pl.semaphore_wait(barrier, 17)
    hist_start()

    r_i = lax.broadcasted_iota(jnp.int32, (SLOTS, SLOTS), 0)
    c_i = lax.broadcasted_iota(jnp.int32, (SLOTS, SLOTS), 1)
    counts = jnp.broadcast_to(counts_ref[...], (SLOTS, SLOTS)).astype(f32)
    slots = jnp.broadcast_to(slot_ref[...], (SLOTS, SLOTS)).astype(f32)
    ends = jnp.sum(jnp.where(c_i <= r_i, counts, 0.0), axis=1, keepdims=True)
    starts = jnp.sum(jnp.where(c_i < r_i, counts, 0.0), axis=1, keepdims=True)
    mine = jnp.sum(jnp.where(c_i == r_i, slots, 0.0), axis=1, keepdims=True)
    r_w = lax.broadcasted_iota(jnp.int32, (SLOTS, 128), 1).astype(f32)
    hit = r_w == mine
    start_row = jnp.sum(jnp.where(hit, starts, 0.0), axis=0, keepdims=True)
    end_row = jnp.sum(jnp.where(hit, ends, 0.0), axis=0, keepdims=True)
    base = (d * C).astype(f32)
    lane = lax.broadcasted_iota(jnp.int32, (CHUNK, 128), 1)
    ones = jnp.where((lane >= SLOTS) & (lane < SLOTS + 3), 1.0, 0.0)
    for r in range(C // CHUNK):
        row = lax.broadcasted_iota(jnp.int32, (CHUNK, 128), 0).astype(f32) + (base + r * CHUNK)
        sel = jnp.where((row >= start_row) & (row < end_row), 1.0, 0.0)
        sel_s[pl.ds(r * CHUNK, CHUNK), :] = (sel + ones).astype(bf16)
        for q in range(CHUNK // 128):
            xt[pl.ds(D, SLOTS), pl.ds(r * CHUNK + q * 128, 128)] = (
                sel[q * 128 : q * 128 + 128].T[:SLOTS].astype(bf16)
            )
    for r in range(8):
        dcol[pl.ds(r * 128, 128), :] = jnp.broadcast_to(dscore_ref[r : r + 1, :], (128, 128)).T

    loads[0].wait()
    loads[1].wait()

    @pl.loop(0, 4)
    def _(k):
        forward(k)

    hist_forward()

    for r in range(4):
        for q in range(4):
            xt[pl.ds(q * 256, 256), pl.ds(r * 256, 256)] = xs[
                pl.ds(r * 256, 256), pl.ds(q * 256, 256)
            ].T

    @pl.loop(4, 8)
    def _(k):
        forward(k)

    hist_recv()

    hgat32[...] = hgat[...].astype(f32).reshape(512, 128)
    for i in range(16):
        for k in range(8):
            h32[pl.ds(4 * i, 4), pl.ds(128 * k, 128)] = hgat32[pl.ds(32 * i + 4 * k, 4), :]
    uh[pl.ds(64, 64), :] = h32[...].astype(bf16)
    loads[2].wait()
    pre = jnp.dot(uh[pl.ds(64, 64), :], we[...], preferred_element_type=f32)
    sig = 0.5 * jnp.tanh(0.5 * pre) + 0.5
    act = pre * sig
    eslope[...] = sig + act * (1.0 - sig)
    uh[pl.ds(0, 64), :] = (h32[...] + act).astype(bf16)

    def group_copy(j):
        y_ = lax.rem(y + j, 4)
        return remote(uh.at[:, ds(y_ * 256, 256)], grx.at[y], g_s.at[j], g_r.at[j], y_peer(j))

    @pl.loop(1, 4)
    def _(j):
        group_copy(j).start()

    grx[y] = uh[:, ds(y * 256, 256)]
    loads[3].wait()

    def core_copy(k):
        return remote(csend.at[k], crecv.at[k], c_s.at[k], c_r.at[k], (g, other))

    def a_copy(k):
        _, x_ = block_of(k)
        return remote(asend.at[k], arecv.at[k], a_s.at[k], a_r.at[k], (g, dev_of(zh, x_)))

    def b_copy(k, j):
        y_ = lax.rem(y + j, 4)
        return remote(bsend.at[k, y_], brecv.at[k, j], b_s.at[k * 4 + j], b_r.at[k * 4 + j], y_peer(j))

    def line_copy(k):
        _, x_ = block_of(k)
        return remote(lsend.at[k], lrecv.at[k], l_s.at[k], l_r.at[k], (g, dev_of(zh, x_)))

    def s_copy():
        return remote(ssend, srecv, s_s.at[0], s_r.at[0], (g, far))

    def a2_copy(kk, j):
        y_ = lax.rem(y + j, 4)
        i = kk * 4 + j
        return remote(a2send.at[kk, y_], a2recv.at[kk, j], a2_s.at[i], a2_r.at[i], y_peer(j))

    def b2_copy(k):
        _, x_ = block_of(k)
        return remote(b2send.at[k], b2recv.at[k], b2_s.at[k], b2_r.at[k], (g, dev_of(zh, x_)))

    def stack(rows, first):
        line = lax.broadcasted_iota(jnp.int32, (16, rows[0].shape[1]), 0)
        out = jnp.zeros((16, rows[0].shape[1]), f32)
        for i, value in enumerate(rows):
            out = jnp.where(line == first + i, value, out)
        return out

    def project(k, picked):
        n = number(k)
        proj = jnp.dot(uh[pl.ds(0, 64), :], both(wu, n), preferred_element_type=f32)
        b0, rest = split(both(bias_ref, n))
        b1, b2 = split(rest)
        picked[pl.ds(0, 64), :] = proj.astype(bf16)
        picked[pl.ds(64, 16), :] = stack([b0, b1, b2], 0).astype(bf16)

    def step(k, z_to, picked, z_from=None, picked_to=None):
        scorer = both(scorer_ref, number(k))
        total = jnp.zeros((8, 256), f32)
        for r in range(C // HALF):
            rows = pl.ds(r * HALF, HALF)
            v = ahead[k, rows, :] + jnp.dot(
                sel_s[rows, :], picked[...], preferred_element_type=f32
            )
            sigma = 0.5 * jnp.tanh(0.5 * v) + 0.5
            hidden = v * sigma
            slope = sigma + hidden * (1.0 - sigma)
            score = dcol[rows, :]
            score = jnp.concatenate([score, score], axis=1)
            z_to[rows, :] = (score * scorer * slope).astype(bf16)
            total = total + jnp.sum((score * hidden).reshape(HALF // 8, 8, 256), axis=0)
            if z_from is not None:
                product(k - 1, r, z_from)
        acts[k] = total
        if picked_to is not None:
            project(k + 1, picked_to)
        if z_from is not None:
            finish(k - 1)

    def product(k, r, z_from):
        rows = pl.ds(r * (ROWS // 2), ROWS // 2)
        term = jnp.dot(xt[rows, :], z_from[...], preferred_element_type=f32)
        part[lax.rem(k, 2), rows, :] = term[:, :128]
        csend[k, rows, :] = term[:, 128:].astype(bf16)

    def finish(k):
        aux = stack(split(jnp.sum(acts[k], axis=0, keepdims=True)), 0)
        part[lax.rem(k, 2), pl.ds(ROWS, 16), :] = aux[:, :128]
        csend[k, pl.ds(ROWS, 16), :] = aux[:, 128:].astype(bf16)
        core_copy(k).start()

    def stage(k):
        core_copy(k).wait_recv()
        total = part[lax.rem(k, 2)] + crecv[k].astype(f32)
        s32[...] = total
        half = total.astype(bf16)
        aux = total[ROWS:]
        tail = stack(split(aux[0:1] + aux[1:2]), 0)

        @pl.when(lax.rem(k, 4) != 3)
        def _():
            lsend[k, pl.ds(0, SLOTS), :] = half[D:ROWS]
            lsend[k, pl.ds(SLOTS, 16), :] = tail.astype(bf16)
            line_copy(k).start()

        for y_ in range(4):
            asend[k, pl.ds(y_ * 128, 128), :] = half[y_ * 256 : y_ * 256 + 128]
            bsend[k, y_] = half[y_ * 256 + 128 : y_ * 256 + 256]

        @pl.loop(1, 4)
        def _(j):
            b_copy(k, j).start()

        @pl.when(lax.rem(k, 4) != 3)
        def _():
            a_copy(k).start()

        @pl.when(lax.rem(k, 4) == 3)
        def _():
            for y_ in range(4):
                aown[lax.div(k, 4), pl.ds(y_ * 128, 128), :] = s32[pl.ds(y_ * 256, 128), :]
            lown[lax.div(k, 4), pl.ds(0, SLOTS), :] = s32[pl.ds(D, SLOTS), :]
            lown[lax.div(k, 4), pl.ds(SLOTS, 16), :] = tail

        bown[k] = s32[pl.ds(pl.multiple_of(y * 256 + 128, 128), 128), :]

    def slot_line(kk):
        total = lown[kk]
        for j in range(3):
            line_copy(4 * kk + j).wait_recv()
            total = total + lrecv[4 * kk + j].astype(f32)
        return total

    def a_second(kk):
        total = aown[kk]
        for j in range(3):
            a_copy(4 * kk + j).wait_recv()
            total = total + arecv[4 * kk + j].astype(f32)
        aown[kk] = total
        half = total.astype(bf16)
        for y_ in range(4):
            a2send[kk, y_] = half[y_ * 128 : y_ * 128 + 128]

        @pl.loop(1, 4)
        def _(j):
            a2_copy(kk, j).start()

    def b_second(k):
        total = bown[k]
        for j in range(1, 4):
            b_copy(k, j).wait_recv()
            total = total + brecv[k, j].astype(f32)
        bown[k] = total
        b2send[k] = total.astype(bf16)

        @pl.when(lax.rem(k, 4) != 3)
        def _():
            b2_copy(k).start()

    for picked in (picked0, picked1):
        picked[pl.ds(64, 64), :] = jnp.zeros((64, 256), bf16)
    project(0, picked0)
    step(0, z0, picked0, None, picked1)

    @pl.loop(0, 3)
    def _(i):
        k = 2 * i
        step(k + 1, z1, picked1, z0, picked0)

        @pl.when(i > 0)
        def _():
            stage(k - 1)

        step(k + 2, z0, picked0, z1, picked1)
        stage(k)

        @pl.when(i == 2)
        def _():
            total = slot_line(0)
            ssend[pl.ds(0, SLOTS), :] = total[:SLOTS].astype(bf16)
            ssend[pl.ds(SLOTS, 16), :] = stack(
                split(total[SLOTS : SLOTS + 1] + total[SLOTS + 1 : SLOTS + 2]), 0
            ).astype(bf16)
            s_copy().start()

    step(7, z1, picked1, z0)
    stage(5)
    for r in range(2):
        product(7, r, z1)
    finish(7)
    stage(6)

    @pl.loop(1, 4)
    def _(j):
        group_copy(j).wait_recv()

    user_cols = grx[:, pl.ds(0, 64), :].reshape(256, 256).T
    hist_cols = grx[:, pl.ds(64, 64), :].reshape(256, 256).T
    stage(7)

    s_copy().wait_recv()
    slot_sum = slot_line(1) + srecv[...].astype(f32)
    rows64 = slot_sum[:SLOTS]
    tail = stack(
        split(jnp.sum(rows64, axis=0, keepdims=True))
        + split(slot_sum[SLOTS : SLOTS + 1] + slot_sum[SLOTS + 1 : SLOTS + 2]),
        0,
    )
    msg[pl.ds(0, SLOTS), :] = rows64.astype(bf16)
    msg[pl.ds(SLOTS, 16), :] = tail.astype(bf16)
    sgf[:, ds(d * 128, 128)] = rows64.astype(bf16)
    slot_start, slot_forward, slot_recv, slot_send = gather(
        lambda i: sgf.at[:, ds(i * 128, 128)], md_s, md_r
    )

    def y_msg(j):
        return remote(msg, mrecv.at[y], my_s.at[j], my_r.at[j], y_peer(j))

    slot_start()

    mrecv[y] = msg[...]

    @pl.loop(1, 4)
    def _(j):
        y_msg(j).start()

    def u_copy(j):
        zl_ = lax.rem(zl + j, 4)
        return remote(usend.at[zl_], urecv.at[j], u_s.at[j], u_r.at[j], z_peer(1, j))

    def t_copy(j):
        return remote(tsend, trecv.at[j], t_s.at[j], t_r.at[j], z_peer(1, j))

    @pl.loop(0, 4)
    def _(k):
        b_second(k)

    a_second(0)
    @pl.loop(1, 4)
    def _(j):
        y_msg(j).wait_recv()

    tails = jnp.sum(mrecv[:, pl.ds(64, 16), :].astype(f32), axis=0)
    tsend[...] = stack([tails[0:1] + tails[1:2], tails[2:3] + tails[3:4]], 0)[:8]

    @pl.loop(1, 4)
    def _(j):
        t_copy(j).start()

    user_part = jnp.dot(
        user_cols, mrecv[:, pl.ds(0, 64), :].reshape(256, 128), preferred_element_type=f32
    ).reshape(4, 64, 128)
    u32[...] = user_part
    usend[...] = user_part.astype(bf16)

    @pl.loop(1, 4)
    def _(j):
        u_copy(j).start()

    @pl.loop(4, 8)
    def _(k):
        b_second(k)

    a_second(1)

    slot_forward()
    slot_recv()
    totals = tsend[...]
    for j in range(1, 4):
        t_copy(j).wait_recv()
        totals = totals + trecv[j]
    frecv[d] = totals
    f_start, f_forward, f_recv, f_send = gather(lambda i: frecv.at[i], f_s, f_r)
    f_start()


    user_grad = lax.dot_general(
        sgf[...], wu[...], (((1,), (1,)), ((), ())), preferred_element_type=f32
    )
    ug32[...] = user_grad
    enc[...] = (user_grad * eslope[...]).astype(bf16)
    own_cols = ds(lax.div(d, 2) * 128, 128)

    def enc_copy(j):
        return remote(enc.at[:, own_cols], erecv.at[y], e_s.at[j], e_r.at[j], y_peer(j))

    @pl.loop(1, 4)
    def _(j):
        enc_copy(j).start()

    erecv[y] = enc[:, own_cols]

    for kk in range(2):
        ta = aown[kk, pl.ds(pl.multiple_of(y * 128, 128), 128), :]
        tb = bown[4 * kk + 3]
        for j in range(1, 4):
            a2_copy(kk, j).wait_recv()
            ta = ta + a2recv[kk, j].astype(f32)
            b2_copy(4 * kk + j - 1).wait_recv()
            tb = tb + b2recv[4 * kk + j - 1].astype(f32)
        for zl_, piece in enumerate((ta[:64], ta[64:], tb[:64], tb[64:])):
            tt32[kk, zl_] = piece
            zsend[kk, zl_] = piece.astype(bf16)

    def z_copy(kk, j):
        zl_ = lax.rem(zl + j, 4)
        i = kk * 4 + j
        return remote(zsend.at[kk, zl_], zrecv.at[kk, j], z_s.at[i], z_r.at[i], z_peer(kk, j))

    z_all = [(0, 0), (0, 1), (0, 2), (0, 3), (1, 1), (1, 2), (1, 3)]
    for kk, j in z_all:
        z_copy(kk, j).start()

    @pl.loop(1, 4)
    def _(j):
        enc_copy(j).wait_recv()

    enc_part = jnp.dot(hist_cols, erecv[...].reshape(256, 128), preferred_element_type=f32)
    enc_part = jnp.where(c == 0, enc_part[:, :64], enc_part[:, 64:]).reshape(4, 2, 32, 64)
    enc_part = jnp.concatenate([enc_part[:, 0], enc_part[:, 1]], axis=2)
    n32[...] = enc_part
    nsend[...] = enc_part.astype(bf16)

    def n_copy(j):
        zl_ = lax.rem(zl + j, 4)
        return remote(nsend.at[zl_], nrecv.at[j], n_s.at[j], n_r.at[j], z_peer(1, j))

    @pl.loop(1, 4)
    def _(j):
        n_copy(j).start()

    f_forward()

    eight = ds(lax.div(d, 2) * 8, 8)
    ug_rows = ug32[eight, :]
    enc_rows = (ug_rows * eslope[eight, :]).astype(bf16)
    hist_grad = ug_rows + lax.dot_general(
        enc_rows, we[...], (((1,), (1,)), ((), ())), preferred_element_type=f32
    )
    hist_grad = jnp.where(c == 0, hist_grad[:4], hist_grad[4:])
    for k in range(8):
        out_ref[pl.ds(224 + 8 * k, 4), :] = hist_grad[:, 128 * k : 128 * k + 128]

    user_out = u32[zl]
    for j in range(1, 4):
        u_copy(j).wait_recv()
        user_out = user_out + urecv[j].astype(f32)
    out_ref[pl.ds(64, 64), :] = user_out

    cand = tt32[1, zl]
    for kk, j in z_all:
        z_copy(kk, j).wait_recv()
        cand = cand + zrecv[kk, j].astype(f32)
    out_ref[pl.ds(0, 64), :] = cand

    enc_out = n32[zl]
    for j in range(1, 4):
        n_copy(j).wait_recv()
        enc_out = enc_out + nrecv[j].astype(f32)
    out_ref[pl.ds(128, 32), pl.ds(0, 64)] = enc_out[:, :64]
    out_ref[pl.ds(160, 32), pl.ds(0, 64)] = enc_out[:, 64:]

    f_recv()

    final = frecv[...]
    out_ref[pl.ds(192, 16), :] = final[:, 1, :]
    out_ref[pl.ds(208, 16), :] = final[:, 0, :]

    hist_send()
    slot_send()
    f_send()
    s_copy().wait_send()

    @pl.loop(0, 8)
    def _(k):
        core_copy(k).wait_send()
        for j in range(1, 4):
            b_copy(k, j).wait_send()

        @pl.when(lax.rem(k, 4) != 3)
        def _():
            a_copy(k).wait_send()
            b2_copy(k).wait_send()
            line_copy(k).wait_send()

    @pl.loop(1, 4)
    def _(j):
        group_copy(j).wait_send()
        y_msg(j).wait_send()
        enc_copy(j).wait_send()
        u_copy(j).wait_send()
        t_copy(j).wait_send()
        n_copy(j).wait_send()
        for kk in range(2):
            a2_copy(kk, j).wait_send()

    for kk, j in z_all:
        z_copy(kk, j).wait_send()


def unpack(packed, cg_ref, ug_ref, eg_ref, sc_ref, bi_ref, hg_ref):
    cg_ref[...] = packed[pl.ds(0, 64), :]
    ug_ref[...] = packed[pl.ds(64, 64), :]
    eg_ref[...] = packed[pl.ds(128, 64), pl.ds(0, 64)]
    sc_ref[...] = packed[pl.ds(192, 16), :]
    bi_ref[...] = packed[pl.ds(208, 16), :]
    for k in range(8):
        hg_ref[0, :, pl.ds(128 * k, 128)] = packed[pl.ds(224 + 8 * k, 4), :]


def local(
    history,
    candidates,
    score_grad,
    req_counts,
    owner_slot,
    encoder_weight,
    user_weight,
    cand_weight,
    hidden_bias,
    scorer_weight,
):
    vmem = pl.BlockSpec(memory_space=pltpu.VMEM)
    hbm = pl.BlockSpec(memory_space=pl.ANY)
    V = pltpu.VMEM
    dma = lambda n: pltpu.SemaphoreType.DMA((n,))
    scratch = [
        V((C, D), bf16),
        V((C, 128), bf16),
        V((ROWS, C), bf16),
        V((D, D), bf16),
        V((D, H), bf16),
        V((D, H), bf16),
        V((C, 128), f32),
        V((8, C, 256), f32),
        V((C, 256), bf16),
        V((C, 256), bf16),
        V((128, 256), bf16),
        V((128, 256), bf16),
        V((8, 8, 256), f32),
        V((32, 128), f32),
        V((16, 32, 128), bf16),
        V((512, 128), f32),
        V((64, D), f32),
        V((128, D), bf16),
        V((64, D), f32),
        V((4, 128, 256), bf16),
        V((2, ROWS + 16, 128), f32),
        V((8, ROWS + 16, 128), bf16),
        V((8, ROWS + 16, 128), bf16),
        V((ROWS + 16, 128), f32),
        V((8, 80, 128), bf16),
        V((8, 80, 128), bf16),
        V((2, 80, 128), f32),
        V((8, 512, 128), bf16),
        V((8, 512, 128), bf16),
        V((2, 512, 128), f32),
        V((8, 4, 128, 128), bf16),
        V((8, 4, 128, 128), bf16),
        V((8, 128, 128), f32),
        V((80, 128), bf16),
        V((80, 128), bf16),
        V((80, 128), bf16),
        V((64, H), bf16),
        V((4, 80, 128), bf16),
        V((2, 4, 128, 128), bf16),
        V((2, 4, 128, 128), bf16),
        V((8, 128, 128), bf16),
        V((8, 128, 128), bf16),
        V((2, 4, 64, 128), f32),
        V((2, 4, 64, 128), bf16),
        V((2, 4, 64, 128), bf16),
        V((64, D), f32),
        V((64, D), bf16),
        V((4, 64, 128), bf16),
        V((4, 64, 128), f32),
        V((4, 64, 128), bf16),
        V((4, 64, 128), bf16),
        V((4, 32, 128), f32),
        V((4, 32, 128), bf16),
        V((4, 32, 128), bf16),
        V((8, 128), f32),
        V((4, 8, 128), f32),
        V((16, 8, 128), f32),
        dma(4),
    ]
    for n in (16, 4, 8, 8, 32, 8, 1, 16, 4, 8, 8, 8, 4, 4, 4, 4, 16):
        scratch += [dma(n), dma(n)]
    packed = pl.pallas_call(
        kernel,
        out_shape=jax.ShapeDtypeStruct((PACKED, 128), f32),
        in_specs=[vmem] * 6 + [hbm] * 4,
        out_specs=vmem,
        scratch_shapes=scratch,
        compiler_params=pltpu.CompilerParams(
            collective_id=0, has_side_effects=True, vmem_limit_bytes=56 * 2**20
        ),
        name="ranking_backward",
    )(
        history,
        score_grad.reshape(8, 128),
        req_counts,
        owner_slot,
        hidden_bias.reshape(1, H),
        scorer_weight.reshape(1, H),
        candidates,
        encoder_weight,
        user_weight,
        cand_weight,
    )
    cg, ug, eg, sc, bi, hg = pl.pallas_call(
        unpack,
        out_shape=(
            jax.ShapeDtypeStruct((64, 128), f32),
            jax.ShapeDtypeStruct((64, 128), f32),
            jax.ShapeDtypeStruct((64, 64), f32),
            jax.ShapeDtypeStruct((16, 128), f32),
            jax.ShapeDtypeStruct((16, 128), f32),
            jax.ShapeDtypeStruct((1, 4, D), f32),
        ),
        in_specs=[vmem],
        out_specs=(vmem,) * 6,
        name="unpack",
    )(packed)
    return (cg, ug, eg, sc.reshape(H), bi.reshape(H), hg)


def solution(mesh):
    in_specs = (
        P("grp", "dev", None),
        P("grp", "dev", None),
        P("grp", "dev"),
        P("grp", None),
        P("grp", None),
        P(),
        P(),
        P(),
        P(),
        P(),
    )
    out_specs = (P("grp", "dev"), P("grp", "dev"), P("grp", "dev"), P(), P(), P("grp", "dev", None))
    return jax.shard_map(local, mesh=mesh, in_specs=in_specs, out_specs=out_specs, check_vma=False)
```

```python
import jax
import jax.numpy as jnp
from jax import lax
from jax.experimental import pallas as pl
from jax.experimental.pallas import tpu as pltpu
from jax.sharding import PartitionSpec as P

f32 = jnp.float32
bf16 = jnp.bfloat16
MESH = pl.DeviceIdType.MESH

D = 1024
H = 2048
C = 1024
SLOTS = 64
ROWS = D + SLOTS
HALF = 512
PACKED = 288
CHUNK = 256


def ds(start, size):
    return pl.ds(pl.multiple_of(start, size), size)


def split(value):
    high = value.astype(bf16).astype(f32)
    return high, value - high


def kernel(
    hist_hbm,
    dscore_hbm,
    counts_hbm,
    slot_hbm,
    bias_hbm,
    scorer_hbm,
    cand_hbm,
    we_hbm,
    wu_hbm,
    wc_hbm,
    out_ref,
    hist_ref,
    dscore_ref,
    counts_ref,
    slot_ref,
    bias_ref,
    scorer_ref,
    xs,
    sel_s,
    xt,
    selt,
    we,
    wu,
    wc,
    dcol,
    ahead,
    z0,
    z1,
    z2,
    picked,
    hp32,
    hgat,
    hgat32,
    h32,
    uh,
    eslope,
    grx,
    part,
    csend,
    crecv,
    s32,
    ahalf,
    bhalf,
    asend,
    arecv,
    aown,
    bsend,
    brecv,
    bown,
    ssend,
    srecv,
    sown,
    msg,
    sgf,
    mrecv,
    a2send,
    a2recv,
    b2send,
    b2recv,
    tt32,
    zsend,
    zrecv,
    enc,
    erecv,
    u32,
    usend,
    urecv,
    n32,
    nsend,
    nrecv,
    tsend,
    trecv,
    frecv,
    ld,
    h_s,
    h_r,
    g_s,
    g_r,
    go_s,
    go_r,
    ah_s,
    ah_r,
    bh_s,
    bh_r,
    c_s,
    c_r,
    a_s,
    a_r,
    b_s,
    b_r,
    s_s,
    s_r,
    md_s,
    md_r,
    my_s,
    my_r,
    a2_s,
    a2_r,
    b2_s,
    b2_r,
    z_s,
    z_r,
    e_s,
    e_r,
    u_s,
    u_r,
    n_s,
    n_r,
    t_s,
    t_r,
    f_s,
    f_r,
):
    g = lax.axis_index("grp")
    d = lax.axis_index("dev")
    y, zl = lax.div(g, 4), lax.rem(g, 4)
    zh, x, c = lax.div(d, 8), lax.rem(lax.div(d, 2), 4), lax.rem(d, 2)
    chip = lax.div(d, 2)
    other = d + 1 - 2 * c

    def dev_of(zh_, x_):
        return zh_ * 8 + x_ * 2 + c

    def chip_peer(j):
        return (g, lax.rem(chip + j, 8) * 2 + c)

    def y_peer(j):
        return (lax.rem(y + j, 4) * 4 + zl, d)

    def z_peer(kk, j):
        return (y * 4 + lax.rem(zl + j, 4), dev_of(lax.rem(zh + 1 + kk, 2), x))

    def block_of(k):
        zh_ = lax.rem(zh + 1 + lax.div(k, 4), 2)
        i = lax.rem(k, 4)
        x_ = lax.rem(x + 2 + 3 * i + 3 * lax.div(i * (i - 1), 2), 4)
        return zh_, x_

    def remote(src, dst, send, recv, to):
        return pltpu.make_async_remote_copy(
            src_ref=src,
            dst_ref=dst,
            send_sem=send,
            recv_sem=recv,
            device_id=to,
            device_id_type=MESH,
        )

    def gather(ref_of, send, recv):
        def own(j):
            return remote(ref_of(d), ref_of(d), send.at[j], recv.at[j], chip_peer(j))

        def beside():
            return remote(ref_of(d), ref_of(d), send.at[0], recv.at[0], (g, other))

        def onward(j):
            i = lax.rem(chip + 8 - j, 8) * 2 + c
            return remote(ref_of(i), ref_of(i), send.at[8 + j], recv.at[8 + j], (g, other))

        def start():
            @pl.loop(1, 8)
            def _(j):
                own(j).start()

            beside().start()

        def forward_all():
            @pl.loop(1, 8)
            def _(j):
                own(j).wait_recv()
                onward(j).start()

        def finish_recv():
            beside().wait_recv()

            @pl.loop(1, 8)
            def _(j):
                onward(j).wait_recv()

        def finish_send():
            beside().wait_send()

            @pl.loop(1, 8)
            def _(j):
                own(j).wait_send()
                onward(j).wait_send()

        return start, forward_all, finish_recv, finish_send

    loads = [
        pltpu.make_async_copy(cand_hbm.at[0], xs, ld.at[0]),
        pltpu.make_async_copy(wc_hbm, wc, ld.at[1]),
        pltpu.make_async_copy(we_hbm, we, ld.at[2]),
        pltpu.make_async_copy(wu_hbm, wu, ld.at[3]),
    ]
    small = [
        pltpu.make_async_copy(src, dst, ld.at[4 + i])
        for i, (src, dst) in enumerate(
            (
                (hist_hbm, hist_ref),
                (dscore_hbm, dscore_ref),
                (counts_hbm, counts_ref),
                (slot_hbm, slot_ref),
                (bias_hbm, bias_ref),
                (scorer_hbm, scorer_ref),
            )
        )
    ]
    for load in small + loads:
        load.start()

    barrier = pltpu.get_barrier_semaphore()

    def greet(to):
        pl.semaphore_signal(barrier, inc=1, device_id=to, device_id_type=MESH)

    @pl.loop(1, 16)
    def _(j):
        greet((g, lax.rem(d + j, 16)))

    @pl.loop(1, 4)
    def _(j):
        greet(z_peer(0, j))
        greet(z_peer(1, j))
        greet(y_peer(j))

    for load in small:
        load.wait()

    hist = hist_ref[0].astype(f32)
    for k in range(8):
        hp32[pl.ds(4 * k, 4), :] = hist[:, 128 * k : 128 * k + 128]
    hgat[d] = hp32[...].astype(bf16)
    hist_start, hist_forward, hist_recv, hist_send = gather(lambda i: hgat.at[i], h_s, h_r)

    def both(ref, n, rows=slice(None)):
        first = ref[rows, ds(n * 256 + c * 128, 128)]
        second = ref[rows, ds(n * 256 + (1 - c) * 128, 128)]
        return jnp.concatenate([first, second], axis=1)

    def number(k):
        zh_, x_ = block_of(k)
        return zh_ * 4 + x_

    def forward(k):
        ahead[k] = jnp.dot(xs[...], both(wc, number(k)), preferred_element_type=f32)

    pl.semaphore_wait(barrier, 24)
    hist_start()

    r_i = lax.broadcasted_iota(jnp.int32, (SLOTS, SLOTS), 0)
    c_i = lax.broadcasted_iota(jnp.int32, (SLOTS, SLOTS), 1)
    counts = jnp.broadcast_to(counts_ref[...], (SLOTS, SLOTS)).astype(f32)
    slots = jnp.broadcast_to(slot_ref[...], (SLOTS, SLOTS)).astype(f32)
    ends = jnp.sum(jnp.where(c_i <= r_i, counts, 0.0), axis=1, keepdims=True)
    starts = jnp.sum(jnp.where(c_i < r_i, counts, 0.0), axis=1, keepdims=True)
    mine = jnp.sum(jnp.where(c_i == r_i, slots, 0.0), axis=1, keepdims=True)
    r_w = lax.broadcasted_iota(jnp.int32, (SLOTS, 128), 1).astype(f32)
    hit = r_w == mine
    start_row = jnp.sum(jnp.where(hit, starts, 0.0), axis=0, keepdims=True)
    end_row = jnp.sum(jnp.where(hit, ends, 0.0), axis=0, keepdims=True)
    base = (d * C).astype(f32)
    lane = lax.broadcasted_iota(jnp.int32, (CHUNK, 128), 1)
    ones = jnp.where((lane >= SLOTS) & (lane < SLOTS + 3), 1.0, 0.0)
    for r in range(C // CHUNK):
        row = lax.broadcasted_iota(jnp.int32, (CHUNK, 128), 0).astype(f32) + (base + r * CHUNK)
        sel = jnp.where((row >= start_row) & (row < end_row), 1.0, 0.0)
        sel_s[pl.ds(r * CHUNK, CHUNK), :] = (sel + ones).astype(bf16)
        for q in range(CHUNK // 128):
            selt[:, pl.ds(r * CHUNK + q * 128, 128)] = (
                sel[q * 128 : q * 128 + 128].T[:SLOTS].astype(bf16)
            )
    for r in range(8):
        dcol[pl.ds(r * 128, 128), :] = jnp.broadcast_to(dscore_ref[r : r + 1, :], (128, 128)).T

    loads[0].wait()
    loads[1].wait()

    @pl.loop(0, 7)
    def _(k):
        forward(k)

    hist_forward()

    for r in range(4):
        for q in range(4):
            xt[pl.ds(q * 256, 256), pl.ds(r * 256, 256)] = xs[
                pl.ds(r * 256, 256), pl.ds(q * 256, 256)
            ].T

    forward(7)

    hist_recv()

    hgat32[...] = hgat[...].astype(f32).reshape(512, 128)
    for i in range(16):
        for k in range(8):
            h32[pl.ds(4 * i, 4), pl.ds(128 * k, 128)] = hgat32[pl.ds(32 * i + 4 * k, 4), :]
    uh[pl.ds(64, 64), :] = h32[...].astype(bf16)
    loads[2].wait()
    pre = jnp.dot(uh[pl.ds(64, 64), :], we[...], preferred_element_type=f32)
    sig = 0.5 * jnp.tanh(0.5 * pre) + 0.5
    act = pre * sig
    eslope[...] = sig + act * (1.0 - sig)
    uh[pl.ds(0, 64), :] = (h32[...] + act).astype(bf16)

    share = pl.ds(pl.multiple_of(c * 64, 64), 64)

    def group_copy(j):
        cols = ds(lax.rem(y + j, 4) * 256, 256)
        return remote(
            uh.at[share, cols], grx.at[y, share], g_s.at[j], g_r.at[j], y_peer(j)
        )

    def group_on(j):
        part_of = grx.at[lax.rem(y + 4 - j, 4), share]
        return remote(part_of, part_of, go_s.at[j], go_r.at[j], (g, other))

    @pl.loop(1, 4)
    def _(j):
        group_copy(j).start()

    grx[y] = uh[:, ds(y * 256, 256)]
    loads[3].wait()

    def core_copy(k):
        return remote(csend.at[k], crecv.at[k], c_s.at[k], c_r.at[k], (g, other))

    def a_copy(k):
        _, x_ = block_of(k)
        return remote(asend.at[k], arecv.at[k], a_s.at[k], a_r.at[k], (g, dev_of(zh, x_)))

    def a_half(i):
        x_ = lax.rem(x + 1 + 2 * i, 4)
        return remote(
            asend.at[0, pl.ds(256 * i, 256)],
            ahalf.at[i],
            ah_s.at[i],
            ah_r.at[i],
            (g, dev_of(zh, x_)),
        )

    def b_half(k, i):
        y_ = lax.rem(y + 2, 4)
        return remote(
            bsend.at[k, y_, pl.ds(64 * i, 64)],
            bhalf.at[k, i],
            bh_s.at[2 * k + i],
            bh_r.at[2 * k + i],
            y_peer(1 + 2 * i),
        )

    def b_copy(k, j):
        y_ = lax.rem(y + j, 4)
        return remote(bsend.at[k, y_], brecv.at[k, j], b_s.at[k * 4 + j], b_r.at[k * 4 + j], y_peer(j))

    def s_copy(k, i):
        zh_, x_ = block_of(k)
        to = zh_ * 8 + x_ * 2 + (c if i == 0 else 1 - c)
        return remote(ssend.at[k, i], srecv.at[k, i], s_s.at[2 * k + i], s_r.at[2 * k + i], (g, to))

    def a2_copy(kk, j):
        y_ = lax.rem(y + j, 4)
        i = kk * 4 + j
        return remote(a2send.at[kk, y_], a2recv.at[kk, j], a2_s.at[i], a2_r.at[i], y_peer(j))

    def b2_copy(k):
        _, x_ = block_of(k)
        return remote(b2send.at[k], b2recv.at[k], b2_s.at[k], b2_r.at[k], (g, dev_of(zh, x_)))

    def stack(rows, first):
        line = lax.broadcasted_iota(jnp.int32, (16, rows[0].shape[1]), 0)
        out = jnp.zeros((16, rows[0].shape[1]), f32)
        for i, value in enumerate(rows):
            out = jnp.where(line == first + i, value, out)
        return out

    def project(k):
        n = number(k)
        proj = jnp.dot(uh[pl.ds(0, 64), :], both(wu, n), preferred_element_type=f32)
        b0, rest = split(both(bias_ref, n))
        b1, b2 = split(rest)
        return proj.astype(bf16), stack([b0, b1, b2], 0).astype(bf16)

    def keep(made):
        picked[pl.ds(0, 64), :] = made[0]
        picked[pl.ds(64, 16), :] = made[1]

    def step(k, z_to, i, z_from=None, first=0):
        scorer = both(scorer_ref, number(k))
        total = jnp.zeros((8, 256), f32)
        made = project(k + 1)
        for r in range(C // HALF):
            rows = pl.ds(r * HALF, HALF)
            v = ahead[k, rows, :] + jnp.dot(
                sel_s[rows, :], picked[...], preferred_element_type=f32
            )
            sigma = 0.5 * jnp.tanh(0.5 * v) + 0.5
            hidden = v * sigma
            slope = sigma + hidden * (1.0 - sigma)
            score = dcol[rows, :]
            score = jnp.concatenate([score, score], axis=1)
            z_to[i, rows, :] = (score * scorer * slope).astype(bf16)
            total = total + jnp.sum((score * hidden).reshape(HALF // 8, 8, 256), axis=0)
            if z_from is not None:
                product(first + i, r, z_from, i)
        keep(made)
        sums = jnp.dot(selt[...], z_to[i], preferred_element_type=f32)
        aux = stack(split(jnp.sum(total, axis=0, keepdims=True)), 0)
        sown[pl.ds(0, SLOTS), :] = sums[:, :128]
        sown[pl.ds(SLOTS, 16), :] = aux[:, :128]
        for q in range(2):
            ssend[k, q, pl.ds(0, SLOTS), :] = sums[:, 128 * q : 128 * q + 128].astype(bf16)
            ssend[k, q, pl.ds(SLOTS, 16), :] = aux[:, 128 * q : 128 * q + 128].astype(bf16)

        @pl.when(k != 7)
        def _():
            s_copy(k, 0).start()

        s_copy(k, 1).start()
        if z_from is not None:
            core_copy(first + i).start()

    def product(k, r, z_from, i):
        rows = pl.ds(r * HALF, HALF)
        term = jnp.dot(xt[rows, :], z_from[i], preferred_element_type=f32)
        part[lax.rem(k, 2), rows, :] = term[:, :128]
        csend[k, rows, :] = term[:, 128:].astype(bf16)

    def back(k, z_from, i):
        for r in range(C // HALF):
            product(k, r, z_from, i)
        core_copy(k).start()

    def stage(k, direct=False):
        core_copy(k).wait_recv()
        now = lax.rem(k, 4)
        kk = lax.div(k, 4)
        total = part[lax.rem(k, 2)] + crecv[k].astype(f32)
        s32[now] = total
        half = total.astype(bf16)
        for y_ in range(4):
            asend[k, pl.ds(y_ * 128, 128), :] = half[y_ * 256 : y_ * 256 + 128]
            bsend[k, y_] = half[y_ * 256 + 128 : y_ * 256 + 256]
        if direct:
            for j in range(1, 4):
                b_copy(k, j).start()
        else:
            for i in range(2):
                b_half(k, i).start()

        bown[k] = s32[now, pl.ds(pl.multiple_of(y * 256 + 128, 128), 128), :]

    def a_keep(kk):
        for y_ in range(4):
            aown[kk, pl.ds(y_ * 128, 128), :] = s32[3, pl.ds(y_ * 256, 128), :]

    def middle(k):
        now = lax.rem(k, 4)
        for i in range(2):
            y_ = lax.rem(y + 1 + 2 * i, 4)
            start = pl.multiple_of(y_ * 256 + 128 + 64 * i, 64)
            b_half(k, i).wait_recv()
            bsend[k, y_, pl.ds(64 * i, 64), :] = (
                s32[now, pl.ds(start, 64), :] + bhalf[k, i].astype(f32)
            ).astype(bf16)
            b_copy(k, 1 + 2 * i).start()

    def a_middle(i):
        a_half(i).wait_recv()
        for y_ in range(2):
            rows = pl.ds(256 * i + 128 * y_, 128)
            more = ahalf[i, pl.ds(128 * y_, 128), :].astype(f32)
            asend[1 + i, rows, :] = (
                s32[1 + i, pl.ds(512 * i + 256 * y_, 128), :] + more
            ).astype(bf16)
        a_copy(1 + i).start()

    def a_second(kk, came):
        total = aown[kk]
        for j in came:
            a_copy(4 * kk + j).wait_recv()
            total = total + arecv[4 * kk + j].astype(f32)
        aown[kk] = total
        half = total.astype(bf16)
        for y_ in range(4):
            a2send[kk, y_] = half[y_ * 128 : y_ * 128 + 128]

        @pl.loop(1, 4)
        def _(j):
            a2_copy(kk, j).start()

    def b_second(k, came=(1, 3)):
        total = bown[k]
        for j in came:
            b_copy(k, j).wait_recv()
            total = total + brecv[k, j].astype(f32)
        bown[k] = total
        b2send[k] = total.astype(bf16)

        @pl.when(lax.rem(k, 4) != 3)
        def _():
            b2_copy(k).start()

    picked[pl.ds(64, 64), :] = jnp.zeros((64, 256), bf16)
    keep(project(0))

    @pl.loop(0, 3)
    def _(i):
        step(i, z0, i)

    @pl.loop(0, 3)
    def _(i):
        step(i + 3, z1, i, z0)

        @pl.when(i > 0)
        def _():
            stage(i - 1)

        @pl.when(i == 0)
        def _():
            @pl.loop(1, 4)
            def _(j):
                group_copy(j).wait_recv()
                group_on(j).start()

        @pl.when(i == 1)
        def _():
            for q in range(2):
                a_half(q).start()

    @pl.loop(0, 2)
    def _(i):
        step(i + 6, z2, i, z1, 3)
        stage(i + 2)
        middle(i)

    a_keep(0)
    a_middle(0)
    a_middle(1)
    back(5, z1, 2)
    stage(4)
    middle(2)

    slot_sum = sown[...]
    for k in range(8):
        for i in range(2):
            if (k, i) != (7, 0):
                s_copy(k, i).wait_recv()
                slot_sum = slot_sum + srecv[k, i].astype(f32)
    rows64 = slot_sum[:SLOTS]
    tail = stack(
        split(jnp.sum(rows64, axis=0, keepdims=True))
        + split(slot_sum[SLOTS : SLOTS + 1] + slot_sum[SLOTS + 1 : SLOTS + 2]),
        0,
    )
    msg[pl.ds(0, SLOTS), :] = rows64.astype(bf16)
    msg[pl.ds(SLOTS, 16), :] = tail.astype(bf16)
    sgf[:, ds(d * 128, 128)] = rows64.astype(bf16)
    slot_start, slot_forward, slot_recv, slot_send = gather(
        lambda i: sgf.at[:, ds(i * 128, 128)], md_s, md_r
    )

    def y_msg(j):
        return remote(msg, mrecv.at[y], my_s.at[j], my_r.at[j], y_peer(j))

    slot_start()

    mrecv[y] = msg[...]

    @pl.loop(1, 4)
    def _(j):
        y_msg(j).start()

    a_copy(4).start()
    back(6, z2, 0)
    stage(5, True)
    a_copy(5).start()
    middle(3)
    back(7, z2, 1)
    stage(6, True)
    a_copy(6).start()
    middle(4)
    stage(7, True)
    a_keep(1)

    @pl.loop(1, 4)
    def _(j):
        group_on(j).wait_recv()

    user_cols = grx[:, pl.ds(0, 64), :].reshape(256, 256).T
    hist_cols = grx[:, pl.ds(64, 64), :].reshape(256, 256).T

    def u_copy(j):
        zl_ = lax.rem(zl + j, 4)
        return remote(usend.at[zl_], urecv.at[j], u_s.at[j], u_r.at[j], z_peer(1, j))

    def t_copy(j):
        return remote(tsend, trecv.at[j], t_s.at[j], t_r.at[j], z_peer(1, j))

    for k in range(3):
        b_second(k)
    slot_forward()
    a_second(0, (1, 2))
    b_second(3)

    @pl.loop(1, 4)
    def _(j):
        y_msg(j).wait_recv()

    tails = jnp.sum(mrecv[:, pl.ds(64, 16), :].astype(f32), axis=0)
    tsend[...] = stack([tails[0:1] + tails[1:2], tails[2:3] + tails[3:4]], 0)[:8]

    @pl.loop(1, 4)
    def _(j):
        t_copy(j).start()

    def z_copy(kk, j):
        zl_ = lax.rem(zl + j, 4)
        i = kk * 4 + j
        return remote(zsend.at[kk, zl_], zrecv.at[kk, j], z_s.at[i], z_r.at[i], z_peer(kk, j))

    z_all = [(0, 0), (0, 1), (0, 2), (0, 3), (1, 1), (1, 2), (1, 3)]

    def last_stage(kk):
        ta = aown[kk, pl.ds(pl.multiple_of(y * 128, 128), 128), :]
        tb = bown[4 * kk + 3]
        for j in range(1, 4):
            a2_copy(kk, j).wait_recv()
            ta = ta + a2recv[kk, j].astype(f32)
            b2_copy(4 * kk + j - 1).wait_recv()
            tb = tb + b2recv[4 * kk + j - 1].astype(f32)
        for zl_, piece in enumerate((ta[:64], ta[64:], tb[:64], tb[64:])):
            tt32[kk, zl_] = piece
            zsend[kk, zl_] = piece.astype(bf16)
        for j in range(kk, 4):
            z_copy(kk, j).start()

    slot_recv()
    own_cols = ds(chip * 128, 128)
    grad_cols = lax.dot_general(
        sgf[...], wu[own_cols, :], (((1,), (1,)), ((), ())), preferred_element_type=f32
    )
    enc[...] = (grad_cols * eslope[:, own_cols]).astype(bf16)

    def enc_copy(j):
        return remote(enc, erecv.at[y], e_s.at[j], e_r.at[j], y_peer(j))

    @pl.loop(1, 4)
    def _(j):
        enc_copy(j).start()

    erecv[y] = enc[...]

    user_part = jnp.dot(
        user_cols, mrecv[:, pl.ds(0, 64), :].reshape(256, 128), preferred_element_type=f32
    ).reshape(4, 64, 128)
    u32[...] = user_part
    usend[...] = user_part.astype(bf16)

    @pl.loop(1, 4)
    def _(j):
        u_copy(j).start()

    totals = tsend[...]
    for j in range(1, 4):
        t_copy(j).wait_recv()
        totals = totals + trecv[j]
    frecv[d] = totals
    f_start, f_forward, f_recv, f_send = gather(lambda i: frecv.at[i], f_s, f_r)
    f_start()

    b_second(4)
    for k in (5, 6, 7):
        b_second(k, (1, 2, 3))
    a_second(1, (0, 1, 2))

    last_stage(0)

    @pl.loop(1, 4)
    def _(j):
        enc_copy(j).wait_recv()

    enc_part = jnp.dot(hist_cols, erecv[...].reshape(256, 128), preferred_element_type=f32)
    enc_part = jnp.where(c == 0, enc_part[:, :64], enc_part[:, 64:]).reshape(4, 2, 32, 64)
    enc_part = jnp.concatenate([enc_part[:, 0], enc_part[:, 1]], axis=2)
    n32[...] = enc_part
    nsend[...] = enc_part.astype(bf16)

    def n_copy(j):
        zl_ = lax.rem(zl + j, 4)
        return remote(nsend.at[zl_], nrecv.at[j], n_s.at[j], n_r.at[j], z_peer(1, j))

    @pl.loop(1, 4)
    def _(j):
        n_copy(j).start()

    last_stage(1)

    sixteen = ds(lax.div(d, 4) * 16, 16)
    grad_rows = lax.dot_general(
        sgf[sixteen, :], wu[...], (((1,), (1,)), ((), ())), preferred_element_type=f32
    )
    enc_rows = (grad_rows * eslope[sixteen, :]).astype(bf16)
    hist_all = grad_rows + lax.dot_general(
        enc_rows, we[...], (((1,), (1,)), ((), ())), preferred_element_type=f32
    )
    place = lax.rem(d, 4)
    hist_grad = hist_all[:4]
    for i in range(1, 4):
        hist_grad = jnp.where(place == i, hist_all[4 * i : 4 * i + 4], hist_grad)
    for k in range(8):
        out_ref[pl.ds(224 + 8 * k, 4), :] = hist_grad[:, 128 * k : 128 * k + 128]

    f_forward()

    user_out = u32[zl]
    for j in range(1, 4):
        u_copy(j).wait_recv()
        user_out = user_out + urecv[j].astype(f32)
    out_ref[pl.ds(64, 64), :] = user_out

    cand = tt32[1, zl]
    for kk, j in z_all:
        z_copy(kk, j).wait_recv()
        cand = cand + zrecv[kk, j].astype(f32)
    out_ref[pl.ds(0, 64), :] = cand

    enc_out = n32[zl]
    for j in range(1, 4):
        n_copy(j).wait_recv()
        enc_out = enc_out + nrecv[j].astype(f32)
    out_ref[pl.ds(128, 32), pl.ds(0, 64)] = enc_out[:, :64]
    out_ref[pl.ds(160, 32), pl.ds(0, 64)] = enc_out[:, 64:]

    f_recv()

    final = frecv[...]
    out_ref[pl.ds(192, 16), :] = final[:, 1, :]
    out_ref[pl.ds(208, 16), :] = final[:, 0, :]

    hist_send()
    slot_send()
    f_send()

    @pl.loop(0, 8)
    def _(k):
        core_copy(k).wait_send()
        s_copy(k, 1).wait_send()

        @pl.when(k != 7)
        def _():
            s_copy(k, 0).wait_send()

        b_copy(k, 1).wait_send()
        b_copy(k, 3).wait_send()

        @pl.when(k < 5)
        def _():
            for i in range(2):
                b_half(k, i).wait_send()

        @pl.when(k >= 5)
        def _():
            b_copy(k, 2).wait_send()

        @pl.when(lax.rem(k, 4) != 3)
        def _():
            b2_copy(k).wait_send()

        @pl.when((lax.rem(k, 4) != 3) & (k > 0))
        def _():
            a_copy(k).wait_send()

    @pl.loop(1, 4)
    def _(j):
        group_copy(j).wait_send()
        group_on(j).wait_send()
        y_msg(j).wait_send()
        enc_copy(j).wait_send()
        u_copy(j).wait_send()
        t_copy(j).wait_send()
        n_copy(j).wait_send()
        for kk in range(2):
            a2_copy(kk, j).wait_send()

    for i in range(2):
        a_half(i).wait_send()

    for kk, j in z_all:
        z_copy(kk, j).wait_send()


def unpack(packed, cg_ref, ug_ref, eg_ref, sc_ref, bi_ref, hg_ref):
    cg_ref[...] = packed[pl.ds(0, 64), :]
    ug_ref[...] = packed[pl.ds(64, 64), :]
    eg_ref[...] = packed[pl.ds(128, 64), pl.ds(0, 64)]
    sc_ref[...] = packed[pl.ds(192, 16), :]
    bi_ref[...] = packed[pl.ds(208, 16), :]
    for k in range(8):
        hg_ref[0, :, pl.ds(128 * k, 128)] = packed[pl.ds(224 + 8 * k, 4), :]


def local(
    history,
    candidates,
    score_grad,
    req_counts,
    owner_slot,
    encoder_weight,
    user_weight,
    cand_weight,
    hidden_bias,
    scorer_weight,
):
    vmem = pl.BlockSpec(memory_space=pltpu.VMEM)
    hbm = pl.BlockSpec(memory_space=pl.ANY)
    V = pltpu.VMEM
    dma = lambda n: pltpu.SemaphoreType.DMA((n,))
    scratch = [
        V((1, 4, D), bf16),
        V((8, 128), f32),
        V((1, SLOTS), jnp.int32),
        V((1, SLOTS), jnp.int32),
        V((1, H), f32),
        V((1, H), f32),
        V((C, D), bf16),
        V((C, 128), bf16),
        V((D, C), bf16),
        V((SLOTS, C), bf16),
        V((D, D), bf16),
        V((D, H), bf16),
        V((D, H), bf16),
        V((C, 128), f32),
        V((8, C, 256), f32),
        V((3, C, 256), bf16),
        V((3, C, 256), bf16),
        V((2, C, 256), bf16),
        V((128, 256), bf16),
        V((32, 128), f32),
        V((16, 32, 128), bf16),
        V((512, 128), f32),
        V((64, D), f32),
        V((128, D), bf16),
        V((64, D), f32),
        V((4, 128, 256), bf16),
        V((2, D, 128), f32),
        V((8, D, 128), bf16),
        V((8, D, 128), bf16),
        V((4, D, 128), f32),
        V((2, 256, 128), bf16),
        V((5, 2, 64, 128), bf16),
        V((8, 512, 128), bf16),
        V((8, 512, 128), bf16),
        V((2, 512, 128), f32),
        V((8, 4, 128, 128), bf16),
        V((8, 4, 128, 128), bf16),
        V((8, 128, 128), f32),
        V((8, 2, 80, 128), bf16),
        V((8, 2, 80, 128), bf16),
        V((80, 128), f32),
        V((80, 128), bf16),
        V((64, H), bf16),
        V((4, 80, 128), bf16),
        V((2, 4, 128, 128), bf16),
        V((2, 4, 128, 128), bf16),
        V((8, 128, 128), bf16),
        V((8, 128, 128), bf16),
        V((2, 4, 64, 128), f32),
        V((2, 4, 64, 128), bf16),
        V((2, 4, 64, 128), bf16),
        V((64, 128), bf16),
        V((4, 64, 128), bf16),
        V((4, 64, 128), f32),
        V((4, 64, 128), bf16),
        V((4, 64, 128), bf16),
        V((4, 32, 128), f32),
        V((4, 32, 128), bf16),
        V((4, 32, 128), bf16),
        V((8, 128), f32),
        V((4, 8, 128), f32),
        V((16, 8, 128), f32),
        dma(10),
    ]
    for n in (16, 4, 4, 2, 10, 8, 8, 32, 16, 16, 4, 8, 8, 8, 4, 4, 4, 4, 16):
        scratch += [dma(n), dma(n)]
    packed = pl.pallas_call(
        kernel,
        out_shape=jax.ShapeDtypeStruct((PACKED, 128), f32),
        in_specs=[hbm] * 10,
        out_specs=vmem,
        scratch_shapes=scratch,
        compiler_params=pltpu.CompilerParams(
            collective_id=0, has_side_effects=True, vmem_limit_bytes=56 * 2**20
        ),
        name="ranking_backward",
    )(
        history,
        score_grad.reshape(8, 128),
        req_counts,
        owner_slot,
        hidden_bias.reshape(1, H),
        scorer_weight.reshape(1, H),
        candidates,
        encoder_weight,
        user_weight,
        cand_weight,
    )
    cg, ug, eg, sc, bi, hg = pl.pallas_call(
        unpack,
        out_shape=(
            jax.ShapeDtypeStruct((64, 128), f32),
            jax.ShapeDtypeStruct((64, 128), f32),
            jax.ShapeDtypeStruct((64, 64), f32),
            jax.ShapeDtypeStruct((16, 128), f32),
            jax.ShapeDtypeStruct((16, 128), f32),
            jax.ShapeDtypeStruct((1, 4, D), f32),
        ),
        in_specs=[vmem],
        out_specs=(vmem,) * 6,
        name="unpack",
    )(packed)
    return (cg, ug, eg, sc.reshape(H), bi.reshape(H), hg)


def solution(mesh):
    in_specs = (
        P("grp", "dev", None),
        P("grp", "dev", None),
        P("grp", "dev"),
        P("grp", None),
        P("grp", None),
        P(),
        P(),
        P(),
        P(),
        P(),
    )
    out_specs = (P("grp", "dev"), P("grp", "dev"), P("grp", "dev"), P(), P(), P("grp", "dev", None))
    return jax.shard_map(local, mesh=mesh, in_specs=in_specs, out_specs=out_specs, check_vma=False)
```

```python
import jax
import jax.numpy as jnp
from jax import lax
from jax.experimental import pallas as pl
from jax.experimental.pallas import tpu as pltpu
from jax.sharding import PartitionSpec as P

f32 = jnp.float32
bf16 = jnp.bfloat16
MESH = pl.DeviceIdType.MESH

D = 1024
H = 2048
C = 1024
SLOTS = 64
ROWS = D + SLOTS
HALF = 512
PACKED = 288
CHUNK = 256


def ds(start, size):
    return pl.ds(pl.multiple_of(start, size), size)


def split(value):
    high = value.astype(bf16).astype(f32)
    return high, value - high


def kernel(
    hist_hbm,
    dscore_hbm,
    counts_hbm,
    slot_hbm,
    bias_hbm,
    scorer_hbm,
    cand_hbm,
    we_hbm,
    wu_hbm,
    wc_hbm,
    out_ref,
    hist_ref,
    dscore_ref,
    counts_ref,
    slot_ref,
    bias_ref,
    scorer_ref,
    xs,
    sel_s,
    xt,
    selt,
    we,
    wu,
    wc,
    dcol,
    ahead,
    z0,
    z1,
    z2,
    picked,
    hp32,
    hgat,
    hgat32,
    h32,
    uh,
    eslope,
    grx,
    part,
    csend,
    crecv,
    s32,
    ahalf,
    bhalf,
    asend,
    arecv,
    aown,
    bsend,
    brecv,
    bown,
    ssend,
    srecv,
    sown,
    msg,
    sgf,
    mrecv,
    a2send,
    a2recv,
    b2send,
    b2recv,
    tt32,
    zsend,
    zrecv,
    enc,
    erecv,
    u32,
    usend,
    urecv,
    n32,
    nsend,
    nrecv,
    tsend,
    trecv,
    frecv,
    ld,
    h_s,
    h_r,
    g_s,
    g_r,
    go_s,
    go_r,
    ah_s,
    ah_r,
    bh_s,
    bh_r,
    c_s,
    c_r,
    a_s,
    a_r,
    b_s,
    b_r,
    s_s,
    s_r,
    md_s,
    md_r,
    my_s,
    my_r,
    a2_s,
    a2_r,
    b2_s,
    b2_r,
    z_s,
    z_r,
    e_s,
    e_r,
    u_s,
    u_r,
    n_s,
    n_r,
    t_s,
    t_r,
    f_s,
    f_r,
):
    g = lax.axis_index("grp")
    d = lax.axis_index("dev")
    y, zl = lax.div(g, 4), lax.rem(g, 4)
    zh, x, c = lax.div(d, 8), lax.rem(lax.div(d, 2), 4), lax.rem(d, 2)
    chip = lax.div(d, 2)
    other = d + 1 - 2 * c

    def dev_of(zh_, x_):
        return zh_ * 8 + x_ * 2 + c

    def chip_peer(j):
        return (g, lax.rem(chip + j, 8) * 2 + c)

    def y_peer(j):
        return (lax.rem(y + j, 4) * 4 + zl, d)

    def z_peer(kk, j):
        return (y * 4 + lax.rem(zl + j, 4), dev_of(lax.rem(zh + 1 + kk, 2), x))

    def block_of(k):
        zh_ = lax.rem(zh + 1 + lax.div(k, 4), 2)
        i = lax.rem(k, 4)
        x_ = lax.rem(x + 2 + 3 * i + 3 * lax.div(i * (i - 1), 2), 4)
        return zh_, x_

    def remote(src, dst, send, recv, to):
        return pltpu.make_async_remote_copy(
            src_ref=src,
            dst_ref=dst,
            send_sem=send,
            recv_sem=recv,
            device_id=to,
            device_id_type=MESH,
        )

    def gather(ref_of, send, recv):
        def own(j):
            return remote(ref_of(d), ref_of(d), send.at[j], recv.at[j], chip_peer(j))

        def beside():
            return remote(ref_of(d), ref_of(d), send.at[0], recv.at[0], (g, other))

        def onward(j):
            i = lax.rem(chip + 8 - j, 8) * 2 + c
            return remote(ref_of(i), ref_of(i), send.at[8 + j], recv.at[8 + j], (g, other))

        def start():
            @pl.loop(1, 8)
            def _(j):
                own(j).start()

            beside().start()

        def forward_all():
            @pl.loop(1, 8)
            def _(j):
                own(j).wait_recv()
                onward(j).start()

        def finish_recv():
            beside().wait_recv()

            @pl.loop(1, 8)
            def _(j):
                onward(j).wait_recv()

        def finish_send():
            beside().wait_send()

            @pl.loop(1, 8)
            def _(j):
                own(j).wait_send()
                onward(j).wait_send()

        return start, forward_all, finish_recv, finish_send

    loads = [
        pltpu.make_async_copy(cand_hbm.at[0], xs, ld.at[0]),
        pltpu.make_async_copy(wc_hbm, wc, ld.at[1]),
        pltpu.make_async_copy(we_hbm, we, ld.at[2]),
        pltpu.make_async_copy(wu_hbm, wu, ld.at[3]),
    ]
    small = [
        pltpu.make_async_copy(src, dst, ld.at[4 + i])
        for i, (src, dst) in enumerate(
            (
                (hist_hbm, hist_ref),
                (dscore_hbm, dscore_ref),
                (counts_hbm, counts_ref),
                (slot_hbm, slot_ref),
                (bias_hbm, bias_ref),
                (scorer_hbm, scorer_ref),
            )
        )
    ]
    for load in small + loads:
        load.start()

    barrier = pltpu.get_barrier_semaphore()

    def greet(to):
        pl.semaphore_signal(barrier, inc=1, device_id=to, device_id_type=MESH)

    @pl.loop(1, 16)
    def _(j):
        greet((g, lax.rem(d + j, 16)))

    @pl.loop(1, 4)
    def _(j):
        greet(z_peer(0, j))
        greet(z_peer(1, j))
        greet(y_peer(j))

    for load in small:
        load.wait()

    hist = hist_ref[0].astype(f32)
    for k in range(8):
        hp32[pl.ds(4 * k, 4), :] = hist[:, 128 * k : 128 * k + 128]
    hgat[d] = hp32[...].astype(bf16)
    hist_start, hist_forward, hist_recv, hist_send = gather(lambda i: hgat.at[i], h_s, h_r)

    def both(ref, n, rows=slice(None)):
        first = ref[rows, ds(n * 256 + c * 128, 128)]
        second = ref[rows, ds(n * 256 + (1 - c) * 128, 128)]
        return jnp.concatenate([first, second], axis=1)

    def number(k):
        zh_, x_ = block_of(k)
        return zh_ * 4 + x_

    def forward(k):
        weights = both(wc, number(k))
        for r in range(C // HALF):
            rows = pl.ds(r * HALF, HALF)
            ahead[k, rows, :] = jnp.dot(xs[rows, :], weights, preferred_element_type=f32)

    pl.semaphore_wait(barrier, 24)
    hist_start()

    r_i = lax.broadcasted_iota(jnp.int32, (SLOTS, SLOTS), 0)
    c_i = lax.broadcasted_iota(jnp.int32, (SLOTS, SLOTS), 1)
    counts = jnp.broadcast_to(counts_ref[...], (SLOTS, SLOTS)).astype(f32)
    slots = jnp.broadcast_to(slot_ref[...], (SLOTS, SLOTS)).astype(f32)
    ends = jnp.sum(jnp.where(c_i <= r_i, counts, 0.0), axis=1, keepdims=True)
    starts = jnp.sum(jnp.where(c_i < r_i, counts, 0.0), axis=1, keepdims=True)
    mine = jnp.sum(jnp.where(c_i == r_i, slots, 0.0), axis=1, keepdims=True)
    r_w = lax.broadcasted_iota(jnp.int32, (SLOTS, 128), 1).astype(f32)
    hit = r_w == mine
    start_row = jnp.sum(jnp.where(hit, starts, 0.0), axis=0, keepdims=True)
    end_row = jnp.sum(jnp.where(hit, ends, 0.0), axis=0, keepdims=True)
    base = (d * C).astype(f32)
    lane = lax.broadcasted_iota(jnp.int32, (CHUNK, 128), 1)
    ones = jnp.where((lane >= SLOTS) & (lane < SLOTS + 3), 1.0, 0.0)
    for r in range(C // CHUNK):
        row = lax.broadcasted_iota(jnp.int32, (CHUNK, 128), 0).astype(f32) + (base + r * CHUNK)
        sel = jnp.where((row >= start_row) & (row < end_row), 1.0, 0.0)
        sel_s[pl.ds(r * CHUNK, CHUNK), :] = (sel + ones).astype(bf16)
        for q in range(CHUNK // 128):
            selt[:, pl.ds(r * CHUNK + q * 128, 128)] = (
                sel[q * 128 : q * 128 + 128].T[:SLOTS].astype(bf16)
            )
    for r in range(8):
        dcol[pl.ds(r * 128, 128), :] = jnp.broadcast_to(dscore_ref[r : r + 1, :], (128, 128)).T

    loads[0].wait()
    loads[1].wait()

    @pl.loop(0, 7)
    def _(k):
        forward(k)

    hist_forward()

    for r in range(4):
        for q in range(4):
            xt[pl.ds(q * 256, 256), pl.ds(r * 256, 256)] = xs[
                pl.ds(r * 256, 256), pl.ds(q * 256, 256)
            ].T

    forward(7)

    hist_recv()

    hgat32[...] = hgat[...].astype(f32).reshape(512, 128)
    for i in range(16):
        for k in range(8):
            h32[pl.ds(4 * i, 4), pl.ds(128 * k, 128)] = hgat32[pl.ds(32 * i + 4 * k, 4), :]
    uh[pl.ds(64, 64), :] = h32[...].astype(bf16)
    loads[2].wait()
    pre = jnp.dot(uh[pl.ds(64, 64), :], we[...], preferred_element_type=f32)
    sig = 0.5 * jnp.tanh(0.5 * pre) + 0.5
    act = pre * sig
    eslope[...] = sig + act * (1.0 - sig)
    uh[pl.ds(0, 64), :] = (h32[...] + act).astype(bf16)

    share = pl.ds(pl.multiple_of(c * 64, 64), 64)

    def group_copy(j):
        cols = ds(lax.rem(y + j, 4) * 256, 256)
        return remote(
            uh.at[share, cols], grx.at[y, share], g_s.at[j], g_r.at[j], y_peer(j)
        )

    def group_on(j):
        part_of = grx.at[lax.rem(y + 4 - j, 4), share]
        return remote(part_of, part_of, go_s.at[j], go_r.at[j], (g, other))

    @pl.loop(1, 4)
    def _(j):
        group_copy(j).start()

    grx[y] = uh[:, ds(y * 256, 256)]
    loads[3].wait()

    def core_copy(k):
        return remote(csend.at[k], crecv.at[k], c_s.at[k], c_r.at[k], (g, other))

    def a_copy(k):
        _, x_ = block_of(k)
        return remote(asend.at[k], arecv.at[k], a_s.at[k], a_r.at[k], (g, dev_of(zh, x_)))

    def a_half(i):
        x_ = lax.rem(x + 1 + 2 * i, 4)
        return remote(
            asend.at[0, pl.ds(256 * i, 256)],
            ahalf.at[i],
            ah_s.at[i],
            ah_r.at[i],
            (g, dev_of(zh, x_)),
        )

    def b_half(k, i):
        y_ = lax.rem(y + 2, 4)
        return remote(
            bsend.at[k, y_, pl.ds(64 * i, 64)],
            bhalf.at[k, i],
            bh_s.at[2 * k + i],
            bh_r.at[2 * k + i],
            y_peer(1 + 2 * i),
        )

    def b_copy(k, j):
        y_ = lax.rem(y + j, 4)
        return remote(bsend.at[k, y_], brecv.at[k, j], b_s.at[k * 4 + j], b_r.at[k * 4 + j], y_peer(j))

    def s_copy(k, i):
        zh_, x_ = block_of(k)
        to = zh_ * 8 + x_ * 2 + (c if i == 0 else 1 - c)
        return remote(ssend.at[k, i], srecv.at[k, i], s_s.at[2 * k + i], s_r.at[2 * k + i], (g, to))

    def a2_copy(kk, j):
        y_ = lax.rem(y + j, 4)
        i = kk * 4 + j
        return remote(a2send.at[kk, y_], a2recv.at[kk, j], a2_s.at[i], a2_r.at[i], y_peer(j))

    def b2_copy(k):
        _, x_ = block_of(k)
        return remote(b2send.at[k], b2recv.at[k], b2_s.at[k], b2_r.at[k], (g, dev_of(zh, x_)))

    def stack(rows, first):
        line = lax.broadcasted_iota(jnp.int32, (16, rows[0].shape[1]), 0)
        out = jnp.zeros((16, rows[0].shape[1]), f32)
        for i, value in enumerate(rows):
            out = jnp.where(line == first + i, value, out)
        return out

    def project(k):
        n = number(k)
        proj = jnp.dot(uh[pl.ds(0, 64), :], both(wu, n), preferred_element_type=f32)
        b0, rest = split(both(bias_ref, n))
        b1, b2 = split(rest)
        return proj.astype(bf16), stack([b0, b1, b2], 0).astype(bf16)

    def keep(made):
        picked[pl.ds(0, 64), :] = made[0]
        picked[pl.ds(64, 16), :] = made[1]

    def step(k, z_to, i, z_from=None, first=0):
        scorer = both(scorer_ref, number(k))
        total = jnp.zeros((8, 256), f32)
        made = project(k + 1)
        for r in range(C // HALF):
            rows = pl.ds(r * HALF, HALF)
            v = ahead[k, rows, :] + jnp.dot(
                sel_s[rows, :], picked[...], preferred_element_type=f32
            )
            sigma = 0.5 * jnp.tanh(0.5 * v) + 0.5
            hidden = v * sigma
            slope = sigma + hidden * (1.0 - sigma)
            score = dcol[rows, :]
            score = jnp.concatenate([score, score], axis=1)
            z_to[i, rows, :] = (score * scorer * slope).astype(bf16)
            total = total + jnp.sum((score * hidden).reshape(HALF // 8, 8, 256), axis=0)
            if z_from is not None:
                product(first + i, r, z_from, i)
        keep(made)
        sums = jnp.dot(selt[...], z_to[i], preferred_element_type=f32)
        aux = stack(split(jnp.sum(total, axis=0, keepdims=True)), 0)
        sown[pl.ds(0, SLOTS), :] = sums[:, :128]
        sown[pl.ds(SLOTS, 16), :] = aux[:, :128]
        for q in range(2):
            ssend[k, q, pl.ds(0, SLOTS), :] = sums[:, 128 * q : 128 * q + 128].astype(bf16)
            ssend[k, q, pl.ds(SLOTS, 16), :] = aux[:, 128 * q : 128 * q + 128].astype(bf16)

        @pl.when(k != 7)
        def _():
            s_copy(k, 0).start()

        s_copy(k, 1).start()
        if z_from is not None:
            core_copy(first + i).start()

    def product(k, r, z_from, i):
        rows = pl.ds(r * HALF, HALF)
        term = jnp.dot(xt[rows, :], z_from[i], preferred_element_type=f32)
        part[lax.rem(k, 2), rows, :] = term[:, :128]
        csend[k, rows, :] = term[:, 128:].astype(bf16)

    def back(k, z_from, i):
        for r in range(C // HALF):
            product(k, r, z_from, i)
        core_copy(k).start()

    def stage(k, direct=False):
        core_copy(k).wait_recv()
        now = lax.rem(k, 4)
        kk = lax.div(k, 4)
        total = part[lax.rem(k, 2)] + crecv[k].astype(f32)
        s32[now] = total
        half = total.astype(bf16)
        for y_ in range(4):
            asend[k, pl.ds(y_ * 128, 128), :] = half[y_ * 256 : y_ * 256 + 128]
            bsend[k, y_] = half[y_ * 256 + 128 : y_ * 256 + 256]
        if direct:
            for j in range(1, 4):
                b_copy(k, j).start()
        else:
            for i in range(2):
                b_half(k, i).start()

        bown[k] = s32[now, pl.ds(pl.multiple_of(y * 256 + 128, 128), 128), :]

    def a_keep(kk):
        for y_ in range(4):
            aown[kk, pl.ds(y_ * 128, 128), :] = s32[3, pl.ds(y_ * 256, 128), :]

    def middle(k):
        now = lax.rem(k, 4)
        for i in range(2):
            y_ = lax.rem(y + 1 + 2 * i, 4)
            start = pl.multiple_of(y_ * 256 + 128 + 64 * i, 64)
            b_half(k, i).wait_recv()
            bsend[k, y_, pl.ds(64 * i, 64), :] = (
                s32[now, pl.ds(start, 64), :] + bhalf[k, i].astype(f32)
            ).astype(bf16)
            b_copy(k, 1 + 2 * i).start()

    def a_middle(i):
        a_half(i).wait_recv()
        for y_ in range(2):
            rows = pl.ds(256 * i + 128 * y_, 128)
            more = ahalf[i, pl.ds(128 * y_, 128), :].astype(f32)
            asend[1 + i, rows, :] = (
                s32[1 + i, pl.ds(512 * i + 256 * y_, 128), :] + more
            ).astype(bf16)
        a_copy(1 + i).start()

    def a_second(kk, came):
        total = aown[kk]
        for j in came:
            a_copy(4 * kk + j).wait_recv()
            total = total + arecv[4 * kk + j].astype(f32)
        aown[kk] = total
        half = total.astype(bf16)
        for y_ in range(4):
            a2send[kk, y_] = half[y_ * 128 : y_ * 128 + 128]

        @pl.loop(1, 4)
        def _(j):
            a2_copy(kk, j).start()

    def b_second(k, came=(1, 3)):
        total = bown[k]
        for j in came:
            b_copy(k, j).wait_recv()
            total = total + brecv[k, j].astype(f32)
        bown[k] = total
        b2send[k] = total.astype(bf16)

        @pl.when(lax.rem(k, 4) != 3)
        def _():
            b2_copy(k).start()

    picked[pl.ds(64, 64), :] = jnp.zeros((64, 256), bf16)
    keep(project(0))

    @pl.loop(0, 3)
    def _(i):
        step(i, z0, i)

    @pl.loop(0, 3)
    def _(i):
        step(i + 3, z1, i, z0)

        @pl.when(i > 0)
        def _():
            stage(i - 1)

        @pl.when(i == 0)
        def _():
            @pl.loop(1, 4)
            def _(j):
                group_copy(j).wait_recv()
                group_on(j).start()

        @pl.when(i == 1)
        def _():
            for q in range(2):
                a_half(q).start()

    @pl.loop(0, 2)
    def _(i):
        step(i + 6, z2, i, z1, 3)
        stage(i + 2)
        middle(i)

    a_keep(0)
    a_middle(0)
    a_middle(1)
    back(5, z1, 2)
    stage(4)
    middle(2)

    slot_sum = sown[...]
    for k in range(8):
        for i in range(2):
            if (k, i) != (7, 0):
                s_copy(k, i).wait_recv()
                slot_sum = slot_sum + srecv[k, i].astype(f32)
    rows64 = slot_sum[:SLOTS]
    tail = stack(
        split(jnp.sum(rows64, axis=0, keepdims=True))
        + split(slot_sum[SLOTS : SLOTS + 1] + slot_sum[SLOTS + 1 : SLOTS + 2]),
        0,
    )
    msg[pl.ds(0, SLOTS), :] = rows64.astype(bf16)
    msg[pl.ds(SLOTS, 16), :] = tail.astype(bf16)
    sgf[:, ds(d * 128, 128)] = rows64.astype(bf16)
    slot_start, slot_forward, slot_recv, slot_send = gather(
        lambda i: sgf.at[:, ds(i * 128, 128)], md_s, md_r
    )

    def y_msg(j):
        return remote(msg, mrecv.at[y], my_s.at[j], my_r.at[j], y_peer(j))

    slot_start()

    mrecv[y] = msg[...]

    @pl.loop(1, 4)
    def _(j):
        y_msg(j).start()

    a_copy(4).start()
    back(6, z2, 0)
    stage(5, True)
    a_copy(5).start()
    middle(3)
    back(7, z2, 1)
    stage(6, True)
    a_copy(6).start()
    middle(4)
    stage(7, True)
    a_keep(1)

    @pl.loop(1, 4)
    def _(j):
        group_on(j).wait_recv()

    user_cols = grx[:, pl.ds(0, 64), :].reshape(256, 256).T
    hist_cols = grx[:, pl.ds(64, 64), :].reshape(256, 256).T

    def u_copy(j):
        zl_ = lax.rem(zl + j, 4)
        return remote(usend.at[zl_], urecv.at[j], u_s.at[j], u_r.at[j], z_peer(1, j))

    def t_copy(j):
        return remote(tsend, trecv.at[j], t_s.at[j], t_r.at[j], z_peer(1, j))

    for k in range(3):
        b_second(k)
    slot_forward()
    a_second(0, (1, 2))
    b_second(3)

    @pl.loop(1, 4)
    def _(j):
        y_msg(j).wait_recv()

    tails = jnp.sum(mrecv[:, pl.ds(64, 16), :].astype(f32), axis=0)
    tsend[...] = stack([tails[0:1] + tails[1:2], tails[2:3] + tails[3:4]], 0)[:8]

    @pl.loop(1, 4)
    def _(j):
        t_copy(j).start()

    def z_copy(kk, j):
        zl_ = lax.rem(zl + j, 4)
        i = kk * 4 + j
        return remote(zsend.at[kk, zl_], zrecv.at[kk, j], z_s.at[i], z_r.at[i], z_peer(kk, j))

    z_all = [(0, 0), (0, 1), (0, 2), (0, 3), (1, 1), (1, 2), (1, 3)]

    def last_stage(kk):
        ta = aown[kk, pl.ds(pl.multiple_of(y * 128, 128), 128), :]
        tb = bown[4 * kk + 3]
        for j in range(1, 4):
            a2_copy(kk, j).wait_recv()
            ta = ta + a2recv[kk, j].astype(f32)
            b2_copy(4 * kk + j - 1).wait_recv()
            tb = tb + b2recv[4 * kk + j - 1].astype(f32)
        for zl_, piece in enumerate((ta[:64], ta[64:], tb[:64], tb[64:])):
            tt32[kk, zl_] = piece
            zsend[kk, zl_] = piece.astype(bf16)
        for j in range(kk, 4):
            z_copy(kk, j).start()

    slot_recv()
    own_cols = ds(chip * 128, 128)
    grad_cols = lax.dot_general(
        sgf[...], wu[own_cols, :], (((1,), (1,)), ((), ())), preferred_element_type=f32
    )
    enc[...] = (grad_cols * eslope[:, own_cols]).astype(bf16)

    def enc_copy(j):
        return remote(enc, erecv.at[y], e_s.at[j], e_r.at[j], y_peer(j))

    @pl.loop(1, 4)
    def _(j):
        enc_copy(j).start()

    erecv[y] = enc[...]

    user_part = jnp.dot(
        user_cols, mrecv[:, pl.ds(0, 64), :].reshape(256, 128), preferred_element_type=f32
    ).reshape(4, 64, 128)
    u32[...] = user_part
    usend[...] = user_part.astype(bf16)

    @pl.loop(1, 4)
    def _(j):
        u_copy(j).start()

    b_second(4)
    for k in (5, 6, 7):
        b_second(k, (1, 2, 3))
    a_second(1, (0, 1, 2))

    totals = tsend[...]
    for j in range(1, 4):
        t_copy(j).wait_recv()
        totals = totals + trecv[j]
    frecv[d] = totals
    f_start, f_forward, f_recv, f_send = gather(lambda i: frecv.at[i], f_s, f_r)
    f_start()

    last_stage(0)

    @pl.loop(1, 4)
    def _(j):
        enc_copy(j).wait_recv()

    enc_part = jnp.dot(hist_cols, erecv[...].reshape(256, 128), preferred_element_type=f32)
    enc_part = jnp.where(c == 0, enc_part[:, :64], enc_part[:, 64:]).reshape(4, 2, 32, 64)
    enc_part = jnp.concatenate([enc_part[:, 0], enc_part[:, 1]], axis=2)
    n32[...] = enc_part
    nsend[...] = enc_part.astype(bf16)

    def n_copy(j):
        zl_ = lax.rem(zl + j, 4)
        return remote(nsend.at[zl_], nrecv.at[j], n_s.at[j], n_r.at[j], z_peer(1, j))

    @pl.loop(1, 4)
    def _(j):
        n_copy(j).start()

    last_stage(1)

    sixteen = ds(lax.div(d, 4) * 16, 16)
    grad_rows = lax.dot_general(
        sgf[sixteen, :], wu[...], (((1,), (1,)), ((), ())), preferred_element_type=f32
    )
    enc_rows = (grad_rows * eslope[sixteen, :]).astype(bf16)
    hist_all = grad_rows + lax.dot_general(
        enc_rows, we[...], (((1,), (1,)), ((), ())), preferred_element_type=f32
    )
    place = lax.rem(d, 4)
    hist_grad = hist_all[:4]
    for i in range(1, 4):
        hist_grad = jnp.where(place == i, hist_all[4 * i : 4 * i + 4], hist_grad)
    for k in range(8):
        out_ref[pl.ds(224 + 8 * k, 4), :] = hist_grad[:, 128 * k : 128 * k + 128]

    f_forward()

    user_out = u32[zl]
    for j in range(1, 4):
        u_copy(j).wait_recv()
        user_out = user_out + urecv[j].astype(f32)
    out_ref[pl.ds(64, 64), :] = user_out

    cand = tt32[1, zl]
    for kk, j in z_all:
        z_copy(kk, j).wait_recv()
        cand = cand + zrecv[kk, j].astype(f32)
    out_ref[pl.ds(0, 64), :] = cand

    enc_out = n32[zl]
    for j in range(1, 4):
        n_copy(j).wait_recv()
        enc_out = enc_out + nrecv[j].astype(f32)
    out_ref[pl.ds(128, 32), pl.ds(0, 64)] = enc_out[:, :64]
    out_ref[pl.ds(160, 32), pl.ds(0, 64)] = enc_out[:, 64:]

    f_recv()

    final = frecv[...]
    out_ref[pl.ds(192, 16), :] = final[:, 1, :]
    out_ref[pl.ds(208, 16), :] = final[:, 0, :]

    hist_send()
    slot_send()
    f_send()

    @pl.loop(0, 8)
    def _(k):
        core_copy(k).wait_send()
        s_copy(k, 1).wait_send()

        @pl.when(k != 7)
        def _():
            s_copy(k, 0).wait_send()

        b_copy(k, 1).wait_send()
        b_copy(k, 3).wait_send()

        @pl.when(k < 5)
        def _():
            for i in range(2):
                b_half(k, i).wait_send()

        @pl.when(k >= 5)
        def _():
            b_copy(k, 2).wait_send()

        @pl.when(lax.rem(k, 4) != 3)
        def _():
            b2_copy(k).wait_send()

        @pl.when((lax.rem(k, 4) != 3) & (k > 0))
        def _():
            a_copy(k).wait_send()

    @pl.loop(1, 4)
    def _(j):
        group_copy(j).wait_send()
        group_on(j).wait_send()
        y_msg(j).wait_send()
        enc_copy(j).wait_send()
        u_copy(j).wait_send()
        t_copy(j).wait_send()
        n_copy(j).wait_send()
        for kk in range(2):
            a2_copy(kk, j).wait_send()

    for i in range(2):
        a_half(i).wait_send()

    for kk, j in z_all:
        z_copy(kk, j).wait_send()


def unpack(packed, cg_ref, ug_ref, eg_ref, sc_ref, bi_ref, hg_ref):
    cg_ref[...] = packed[pl.ds(0, 64), :]
    ug_ref[...] = packed[pl.ds(64, 64), :]
    eg_ref[...] = packed[pl.ds(128, 64), pl.ds(0, 64)]
    sc_ref[...] = packed[pl.ds(192, 16), :]
    bi_ref[...] = packed[pl.ds(208, 16), :]
    for k in range(8):
        hg_ref[0, :, pl.ds(128 * k, 128)] = packed[pl.ds(224 + 8 * k, 4), :]


def local(
    history,
    candidates,
    score_grad,
    req_counts,
    owner_slot,
    encoder_weight,
    user_weight,
    cand_weight,
    hidden_bias,
    scorer_weight,
):
    vmem = pl.BlockSpec(memory_space=pltpu.VMEM)
    hbm = pl.BlockSpec(memory_space=pl.ANY)
    V = pltpu.VMEM
    dma = lambda n: pltpu.SemaphoreType.DMA((n,))
    scratch = [
        V((1, 4, D), bf16),
        V((8, 128), f32),
        V((1, SLOTS), jnp.int32),
        V((1, SLOTS), jnp.int32),
        V((1, H), f32),
        V((1, H), f32),
        V((C, D), bf16),
        V((C, 128), bf16),
        V((D, C), bf16),
        V((SLOTS, C), bf16),
        V((D, D), bf16),
        V((D, H), bf16),
        V((D, H), bf16),
        V((C, 128), f32),
        V((8, C, 256), f32),
        V((3, C, 256), bf16),
        V((3, C, 256), bf16),
        V((2, C, 256), bf16),
        V((128, 256), bf16),
        V((32, 128), f32),
        V((16, 32, 128), bf16),
        V((512, 128), f32),
        V((64, D), f32),
        V((128, D), bf16),
        V((64, D), f32),
        V((4, 128, 256), bf16),
        V((2, D, 128), f32),
        V((8, D, 128), bf16),
        V((8, D, 128), bf16),
        V((4, D, 128), f32),
        V((2, 256, 128), bf16),
        V((5, 2, 64, 128), bf16),
        V((8, 512, 128), bf16),
        V((8, 512, 128), bf16),
        V((2, 512, 128), f32),
        V((8, 4, 128, 128), bf16),
        V((8, 4, 128, 128), bf16),
        V((8, 128, 128), f32),
        V((8, 2, 80, 128), bf16),
        V((8, 2, 80, 128), bf16),
        V((80, 128), f32),
        V((80, 128), bf16),
        V((64, H), bf16),
        V((4, 80, 128), bf16),
        V((2, 4, 128, 128), bf16),
        V((2, 4, 128, 128), bf16),
        V((8, 128, 128), bf16),
        V((8, 128, 128), bf16),
        V((2, 4, 64, 128), f32),
        V((2, 4, 64, 128), bf16),
        V((2, 4, 64, 128), bf16),
        V((64, 128), bf16),
        V((4, 64, 128), bf16),
        V((4, 64, 128), f32),
        V((4, 64, 128), bf16),
        V((4, 64, 128), bf16),
        V((4, 32, 128), f32),
        V((4, 32, 128), bf16),
        V((4, 32, 128), bf16),
        V((8, 128), f32),
        V((4, 8, 128), f32),
        V((16, 8, 128), f32),
        dma(10),
    ]
    for n in (16, 4, 4, 2, 10, 8, 8, 32, 16, 16, 4, 8, 8, 8, 4, 4, 4, 4, 16):
        scratch += [dma(n), dma(n)]
    packed = pl.pallas_call(
        kernel,
        out_shape=jax.ShapeDtypeStruct((PACKED, 128), f32),
        in_specs=[hbm] * 10,
        out_specs=vmem,
        scratch_shapes=scratch,
        compiler_params=pltpu.CompilerParams(
            collective_id=0, has_side_effects=True, vmem_limit_bytes=56 * 2**20
        ),
        name="ranking_backward",
    )(
        history,
        score_grad.reshape(8, 128),
        req_counts,
        owner_slot,
        hidden_bias.reshape(1, H),
        scorer_weight.reshape(1, H),
        candidates,
        encoder_weight,
        user_weight,
        cand_weight,
    )
    cg, ug, eg, sc, bi, hg = pl.pallas_call(
        unpack,
        out_shape=(
            jax.ShapeDtypeStruct((64, 128), f32),
            jax.ShapeDtypeStruct((64, 128), f32),
            jax.ShapeDtypeStruct((64, 64), f32),
            jax.ShapeDtypeStruct((16, 128), f32),
            jax.ShapeDtypeStruct((16, 128), f32),
            jax.ShapeDtypeStruct((1, 4, D), f32),
        ),
        in_specs=[vmem],
        out_specs=(vmem,) * 6,
        name="unpack",
    )(packed)
    return (cg, ug, eg, sc.reshape(H), bi.reshape(H), hg)


def solution(mesh):
    in_specs = (
        P("grp", "dev", None),
        P("grp", "dev", None),
        P("grp", "dev"),
        P("grp", None),
        P("grp", None),
        P(),
        P(),
        P(),
        P(),
        P(),
    )
    out_specs = (P("grp", "dev"), P("grp", "dev"), P("grp", "dev"), P(), P(), P("grp", "dev", None))
    return jax.shard_map(local, mesh=mesh, in_specs=in_specs, out_specs=out_specs, check_vma=False)
```

```python
import jax
import jax.numpy as jnp
from jax import lax
from jax.experimental import pallas as pl
from jax.experimental.pallas import tpu as pltpu
from jax.sharding import PartitionSpec as P

f32 = jnp.float32
bf16 = jnp.bfloat16
MESH = pl.DeviceIdType.MESH

D = 1024
H = 2048
C = 1024
SLOTS = 64
ROWS = D + SLOTS
HALF = 512
PACKED = 288
CHUNK = 256


def ds(start, size):
    return pl.ds(pl.multiple_of(start, size), size)


def split(value):
    high = value.astype(bf16).astype(f32)
    return high, value - high


def kernel(
    hist_hbm,
    dscore_hbm,
    counts_hbm,
    slot_hbm,
    bias_hbm,
    scorer_hbm,
    cand_hbm,
    we_hbm,
    wu_hbm,
    wc_hbm,
    out_ref,
    hist_ref,
    dscore_ref,
    counts_ref,
    slot_ref,
    bias_ref,
    scorer_ref,
    xs,
    sel_s,
    xt,
    selt,
    we,
    wu,
    wc,
    dcol,
    ahead,
    z0,
    z1,
    z2,
    picked,
    hp32,
    hgat,
    hgat32,
    h32,
    uh,
    eslope,
    grx,
    part,
    csend,
    crecv,
    s32,
    ahalf,
    bhalf,
    asend,
    arecv,
    aown,
    bsend,
    brecv,
    bown,
    ssend,
    srecv,
    sown,
    msg,
    sgf,
    mrecv,
    a2send,
    a2recv,
    b2send,
    b2recv,
    tt32,
    zsend,
    zrecv,
    enc,
    erecv,
    u32,
    usend,
    urecv,
    n32,
    nsend,
    nrecv,
    tsend,
    trecv,
    frecv,
    ld,
    h_s,
    h_r,
    g_s,
    g_r,
    go_s,
    go_r,
    ah_s,
    ah_r,
    bh_s,
    bh_r,
    c_s,
    c_r,
    a_s,
    a_r,
    b_s,
    b_r,
    s_s,
    s_r,
    md_s,
    md_r,
    my_s,
    my_r,
    a2_s,
    a2_r,
    b2_s,
    b2_r,
    z_s,
    z_r,
    e_s,
    e_r,
    u_s,
    u_r,
    n_s,
    n_r,
    t_s,
    t_r,
    f_s,
    f_r,
):
    g = lax.axis_index("grp")
    d = lax.axis_index("dev")
    y, zl = lax.div(g, 4), lax.rem(g, 4)
    zh, x, c = lax.div(d, 8), lax.rem(lax.div(d, 2), 4), lax.rem(d, 2)
    chip = lax.div(d, 2)
    other = d + 1 - 2 * c

    def dev_of(zh_, x_):
        return zh_ * 8 + x_ * 2 + c

    def chip_peer(j):
        return (g, lax.rem(chip + j, 8) * 2 + c)

    def y_peer(j):
        return (lax.rem(y + j, 4) * 4 + zl, d)

    def z_peer(kk, j):
        return (y * 4 + lax.rem(zl + j, 4), dev_of(lax.rem(zh + 1 + kk, 2), x))

    def block_of(k):
        zh_ = lax.rem(zh + 1 + lax.div(k, 4), 2)
        i = lax.rem(k, 4)
        x_ = lax.rem(x + 2 + 3 * i + 3 * lax.div(i * (i - 1), 2), 4)
        return zh_, x_

    def remote(src, dst, send, recv, to):
        return pltpu.make_async_remote_copy(
            src_ref=src,
            dst_ref=dst,
            send_sem=send,
            recv_sem=recv,
            device_id=to,
            device_id_type=MESH,
        )

    def gather(ref_of, send, recv):
        def own(j):
            return remote(ref_of(d), ref_of(d), send.at[j], recv.at[j], chip_peer(j))

        def beside():
            return remote(ref_of(d), ref_of(d), send.at[0], recv.at[0], (g, other))

        def onward(j):
            i = lax.rem(chip + 8 - j, 8) * 2 + c
            return remote(ref_of(i), ref_of(i), send.at[8 + j], recv.at[8 + j], (g, other))

        def start():
            @pl.loop(1, 8)
            def _(j):
                own(j).start()

            beside().start()

        def forward_all():
            @pl.loop(1, 8)
            def _(j):
                own(j).wait_recv()
                onward(j).start()

        def finish_recv():
            beside().wait_recv()

            @pl.loop(1, 8)
            def _(j):
                onward(j).wait_recv()

        def finish_send():
            beside().wait_send()

            @pl.loop(1, 8)
            def _(j):
                own(j).wait_send()
                onward(j).wait_send()

        return start, forward_all, finish_recv, finish_send

    loads = [
        pltpu.make_async_copy(cand_hbm.at[0], xs, ld.at[0]),
        pltpu.make_async_copy(wc_hbm, wc, ld.at[1]),
        pltpu.make_async_copy(we_hbm, we, ld.at[2]),
        pltpu.make_async_copy(wu_hbm, wu, ld.at[3]),
    ]
    small = [
        pltpu.make_async_copy(src, dst, ld.at[4 + i])
        for i, (src, dst) in enumerate(
            (
                (hist_hbm, hist_ref),
                (dscore_hbm, dscore_ref),
                (counts_hbm, counts_ref),
                (slot_hbm, slot_ref),
                (bias_hbm, bias_ref),
                (scorer_hbm, scorer_ref),
            )
        )
    ]
    for load in small + loads:
        load.start()

    barrier = pltpu.get_barrier_semaphore()

    def greet(to):
        pl.semaphore_signal(barrier, inc=1, device_id=to, device_id_type=MESH)

    @pl.loop(1, 16)
    def _(j):
        greet((g, lax.rem(d + j, 16)))

    @pl.loop(1, 4)
    def _(j):
        greet(z_peer(0, j))
        greet(z_peer(1, j))
        greet(y_peer(j))

    for load in small:
        load.wait()

    hist = hist_ref[0].astype(f32)
    for k in range(8):
        hp32[pl.ds(4 * k, 4), :] = hist[:, 128 * k : 128 * k + 128]
    hgat[d] = hp32[...].astype(bf16)
    hist_start, hist_forward, hist_recv, hist_send = gather(lambda i: hgat.at[i], h_s, h_r)

    def both(ref, n, rows=slice(None)):
        first = ref[rows, ds(n * 256 + c * 128, 128)]
        second = ref[rows, ds(n * 256 + (1 - c) * 128, 128)]
        return jnp.concatenate([first, second], axis=1)

    def number(k):
        zh_, x_ = block_of(k)
        return zh_ * 4 + x_

    def forward(k):
        weights = both(wc, number(k))
        for r in range(C // HALF):
            rows = pl.ds(r * HALF, HALF)
            ahead[k, rows, :] = jnp.dot(xs[rows, :], weights, preferred_element_type=f32)

    pl.semaphore_wait(barrier, 24)
    hist_start()

    r_i = lax.broadcasted_iota(jnp.int32, (SLOTS, SLOTS), 0)
    c_i = lax.broadcasted_iota(jnp.int32, (SLOTS, SLOTS), 1)
    counts = jnp.broadcast_to(counts_ref[...], (SLOTS, SLOTS)).astype(f32)
    slots = jnp.broadcast_to(slot_ref[...], (SLOTS, SLOTS)).astype(f32)
    ends = jnp.sum(jnp.where(c_i <= r_i, counts, 0.0), axis=1, keepdims=True)
    starts = jnp.sum(jnp.where(c_i < r_i, counts, 0.0), axis=1, keepdims=True)
    mine = jnp.sum(jnp.where(c_i == r_i, slots, 0.0), axis=1, keepdims=True)
    r_w = lax.broadcasted_iota(jnp.int32, (SLOTS, 128), 1).astype(f32)
    hit = r_w == mine
    start_row = jnp.sum(jnp.where(hit, starts, 0.0), axis=0, keepdims=True)
    end_row = jnp.sum(jnp.where(hit, ends, 0.0), axis=0, keepdims=True)
    base = (d * C).astype(f32)
    lane = lax.broadcasted_iota(jnp.int32, (CHUNK, 128), 1)
    ones = jnp.where((lane >= SLOTS) & (lane < SLOTS + 3), 1.0, 0.0)
    for r in range(C // CHUNK):
        row = lax.broadcasted_iota(jnp.int32, (CHUNK, 128), 0).astype(f32) + (base + r * CHUNK)
        sel = jnp.where((row >= start_row) & (row < end_row), 1.0, 0.0)
        sel_s[pl.ds(r * CHUNK, CHUNK), :] = (sel + ones).astype(bf16)
        for q in range(CHUNK // 128):
            selt[:, pl.ds(r * CHUNK + q * 128, 128)] = (
                sel[q * 128 : q * 128 + 128].T[:SLOTS].astype(bf16)
            )
    for r in range(8):
        dcol[pl.ds(r * 128, 128), :] = jnp.broadcast_to(dscore_ref[r : r + 1, :], (128, 128)).T

    loads[0].wait()
    loads[1].wait()

    @pl.loop(0, 7)
    def _(k):
        forward(k)

    hist_forward()

    for r in range(4):
        for q in range(4):
            xt[pl.ds(q * 256, 256), pl.ds(r * 256, 256)] = xs[
                pl.ds(r * 256, 256), pl.ds(q * 256, 256)
            ].T

    forward(7)

    hist_recv()

    hgat32[...] = hgat[...].astype(f32).reshape(512, 128)
    for i in range(16):
        for k in range(8):
            h32[pl.ds(4 * i, 4), pl.ds(128 * k, 128)] = hgat32[pl.ds(32 * i + 4 * k, 4), :]
    uh[pl.ds(64, 64), :] = h32[...].astype(bf16)
    loads[2].wait()
    pre = jnp.dot(uh[pl.ds(64, 64), :], we[...], preferred_element_type=f32)
    sig = 0.5 * jnp.tanh(0.5 * pre) + 0.5
    act = pre * sig
    eslope[...] = sig + act * (1.0 - sig)
    uh[pl.ds(0, 64), :] = (h32[...] + act).astype(bf16)

    share = pl.ds(pl.multiple_of(c * 64, 64), 64)

    def group_copy(j):
        cols = ds(lax.rem(y + j, 4) * 256, 256)
        return remote(
            uh.at[share, cols], grx.at[y, share], g_s.at[j], g_r.at[j], y_peer(j)
        )

    def group_on(j):
        part_of = grx.at[lax.rem(y + 4 - j, 4), share]
        return remote(part_of, part_of, go_s.at[j], go_r.at[j], (g, other))

    @pl.loop(1, 4)
    def _(j):
        group_copy(j).start()

    grx[y] = uh[:, ds(y * 256, 256)]
    loads[3].wait()

    def core_copy(k):
        return remote(csend.at[k], crecv.at[k], c_s.at[k], c_r.at[k], (g, other))

    def a_copy(k):
        _, x_ = block_of(k)
        return remote(asend.at[k], arecv.at[k], a_s.at[k], a_r.at[k], (g, dev_of(zh, x_)))

    def a_half(i):
        x_ = lax.rem(x + 1 + 2 * i, 4)
        return remote(
            asend.at[0, pl.ds(256 * i, 256)],
            ahalf.at[i],
            ah_s.at[i],
            ah_r.at[i],
            (g, dev_of(zh, x_)),
        )

    def b_half(k, i):
        y_ = lax.rem(y + 2, 4)
        return remote(
            bsend.at[k, y_, pl.ds(64 * i, 64)],
            bhalf.at[k, i],
            bh_s.at[2 * k + i],
            bh_r.at[2 * k + i],
            y_peer(1 + 2 * i),
        )

    def b_copy(k, j):
        y_ = lax.rem(y + j, 4)
        return remote(bsend.at[k, y_], brecv.at[k, j], b_s.at[k * 4 + j], b_r.at[k * 4 + j], y_peer(j))

    def s_copy(k, i):
        zh_, x_ = block_of(k)
        to = zh_ * 8 + x_ * 2 + (c if i == 0 else 1 - c)
        return remote(ssend.at[k, i], srecv.at[k, i], s_s.at[2 * k + i], s_r.at[2 * k + i], (g, to))

    def a2_copy(kk, j):
        y_ = lax.rem(y + j, 4)
        i = kk * 4 + j
        return remote(a2send.at[kk, y_], a2recv.at[kk, j], a2_s.at[i], a2_r.at[i], y_peer(j))

    def b2_copy(k):
        _, x_ = block_of(k)
        return remote(b2send.at[k], b2recv.at[k], b2_s.at[k], b2_r.at[k], (g, dev_of(zh, x_)))

    def stack(rows, first):
        line = lax.broadcasted_iota(jnp.int32, (16, rows[0].shape[1]), 0)
        out = jnp.zeros((16, rows[0].shape[1]), f32)
        for i, value in enumerate(rows):
            out = jnp.where(line == first + i, value, out)
        return out

    def project(k):
        n = number(k)
        proj = jnp.dot(uh[pl.ds(0, 64), :], both(wu, n), preferred_element_type=f32)
        b0, rest = split(both(bias_ref, n))
        b1, b2 = split(rest)
        return proj.astype(bf16), stack([b0, b1, b2], 0).astype(bf16)

    def keep(made):
        picked[pl.ds(0, 64), :] = made[0]
        picked[pl.ds(64, 16), :] = made[1]

    def step(k, z_to, i, z_from=None, first=0):
        scorer = both(scorer_ref, number(k))
        total = jnp.zeros((8, 256), f32)
        made = project(k + 1)
        for r in range(C // HALF):
            rows = pl.ds(r * HALF, HALF)
            v = ahead[k, rows, :] + jnp.dot(
                sel_s[rows, :], picked[...], preferred_element_type=f32
            )
            sigma = 0.5 * jnp.tanh(0.5 * v) + 0.5
            hidden = v * sigma
            slope = sigma + hidden * (1.0 - sigma)
            score = dcol[rows, :]
            score = jnp.concatenate([score, score], axis=1)
            z_to[i, rows, :] = (score * scorer * slope).astype(bf16)
            total = total + jnp.sum((score * hidden).reshape(HALF // 8, 8, 256), axis=0)
            if z_from is not None:
                product(first + i, r, z_from, i)
        keep(made)
        sums = jnp.dot(selt[...], z_to[i], preferred_element_type=f32)
        aux = stack(split(jnp.sum(total, axis=0, keepdims=True)), 0)
        sown[pl.ds(0, SLOTS), :] = sums[:, :128]
        sown[pl.ds(SLOTS, 16), :] = aux[:, :128]
        for q in range(2):
            ssend[k, q, pl.ds(0, SLOTS), :] = sums[:, 128 * q : 128 * q + 128].astype(bf16)
            ssend[k, q, pl.ds(SLOTS, 16), :] = aux[:, 128 * q : 128 * q + 128].astype(bf16)

        @pl.when(k != 7)
        def _():
            s_copy(k, 0).start()

        s_copy(k, 1).start()
        if z_from is not None:
            core_copy(first + i).start()

    def product(k, r, z_from, i):
        rows = pl.ds(r * HALF, HALF)
        term = jnp.dot(xt[rows, :], z_from[i], preferred_element_type=f32)
        part[lax.rem(k, 2), rows, :] = term[:, :128]
        csend[k, rows, :] = term[:, 128:].astype(bf16)

    def back(k, z_from, i):
        for r in range(C // HALF):
            product(k, r, z_from, i)
        core_copy(k).start()

    def stage(k, direct=False):
        core_copy(k).wait_recv()
        now = lax.rem(k, 4)
        kk = lax.div(k, 4)
        total = part[lax.rem(k, 2)] + crecv[k].astype(f32)
        s32[now] = total
        half = total.astype(bf16)
        for y_ in range(4):
            asend[k, pl.ds(y_ * 128, 128), :] = half[y_ * 256 : y_ * 256 + 128]
            bsend[k, y_] = half[y_ * 256 + 128 : y_ * 256 + 256]
        if direct:
            for j in range(1, 4):
                b_copy(k, j).start()
        else:
            for i in range(2):
                b_half(k, i).start()

        bown[k] = s32[now, pl.ds(pl.multiple_of(y * 256 + 128, 128), 128), :]

    def a_keep(kk):
        for y_ in range(4):
            aown[kk, pl.ds(y_ * 128, 128), :] = s32[3, pl.ds(y_ * 256, 128), :]

    def middle(k):
        now = lax.rem(k, 4)
        for i in range(2):
            y_ = lax.rem(y + 1 + 2 * i, 4)
            start = pl.multiple_of(y_ * 256 + 128 + 64 * i, 64)
            b_half(k, i).wait_recv()
            bsend[k, y_, pl.ds(64 * i, 64), :] = (
                s32[now, pl.ds(start, 64), :] + bhalf[k, i].astype(f32)
            ).astype(bf16)
            b_copy(k, 1 + 2 * i).start()

    def a_middle(i):
        a_half(i).wait_recv()
        for y_ in range(2):
            rows = pl.ds(256 * i + 128 * y_, 128)
            more = ahalf[i, pl.ds(128 * y_, 128), :].astype(f32)
            asend[1 + i, rows, :] = (
                s32[1 + i, pl.ds(512 * i + 256 * y_, 128), :] + more
            ).astype(bf16)
        a_copy(1 + i).start()

    def a_second(kk, came):
        total = aown[kk]
        for j in came:
            a_copy(4 * kk + j).wait_recv()
            total = total + arecv[4 * kk + j].astype(f32)
        aown[kk] = total
        half = total.astype(bf16)
        for y_ in range(4):
            a2send[kk, y_] = half[y_ * 128 : y_ * 128 + 128]

        @pl.loop(1, 4)
        def _(j):
            a2_copy(kk, j).start()

    def b_second(k, came=(1, 3)):
        total = bown[k]
        for j in came:
            b_copy(k, j).wait_recv()
            total = total + brecv[k, j].astype(f32)
        bown[k] = total
        b2send[k] = total.astype(bf16)

        @pl.when(lax.rem(k, 4) != 3)
        def _():
            b2_copy(k).start()

    picked[pl.ds(64, 64), :] = jnp.zeros((64, 256), bf16)
    keep(project(0))

    @pl.loop(0, 3)
    def _(i):
        step(i, z0, i)

    @pl.loop(0, 3)
    def _(i):
        step(i + 3, z1, i, z0)

        @pl.when(i > 0)
        def _():
            stage(i - 1)

        @pl.when(i == 0)
        def _():
            @pl.loop(1, 4)
            def _(j):
                group_copy(j).wait_recv()
                group_on(j).start()

        @pl.when(i == 1)
        def _():
            for q in range(2):
                a_half(q).start()

    @pl.loop(0, 2)
    def _(i):
        step(i + 6, z2, i, z1, 3)
        stage(i + 2)
        middle(i)

    a_keep(0)
    a_middle(0)
    a_middle(1)
    back(5, z1, 2)
    stage(4)
    middle(2)

    slot_sum = sown[...]
    for k in range(8):
        for i in range(2):
            if (k, i) != (7, 0):
                s_copy(k, i).wait_recv()
                slot_sum = slot_sum + srecv[k, i].astype(f32)
    rows64 = slot_sum[:SLOTS]
    tail = stack(
        split(jnp.sum(rows64, axis=0, keepdims=True))
        + split(slot_sum[SLOTS : SLOTS + 1] + slot_sum[SLOTS + 1 : SLOTS + 2]),
        0,
    )
    msg[pl.ds(0, SLOTS), :] = rows64.astype(bf16)
    msg[pl.ds(SLOTS, 16), :] = tail.astype(bf16)
    sgf[:, ds(d * 128, 128)] = rows64.astype(bf16)
    slot_start, slot_forward, slot_recv, slot_send = gather(
        lambda i: sgf.at[:, ds(i * 128, 128)], md_s, md_r
    )

    def y_msg(j):
        return remote(msg, mrecv.at[y], my_s.at[j], my_r.at[j], y_peer(j))

    slot_start()

    mrecv[y] = msg[...]

    @pl.loop(1, 4)
    def _(j):
        y_msg(j).start()

    back(6, z2, 0)
    stage(5, True)
    a_copy(4).start()
    a_copy(5).start()
    middle(3)
    back(7, z2, 1)
    stage(6, True)
    a_copy(6).start()
    middle(4)
    stage(7, True)
    a_keep(1)

    @pl.loop(1, 4)
    def _(j):
        group_on(j).wait_recv()

    user_cols = grx[:, pl.ds(0, 64), :].reshape(256, 256).T
    hist_cols = grx[:, pl.ds(64, 64), :].reshape(256, 256).T

    def u_copy(j):
        zl_ = lax.rem(zl + j, 4)
        return remote(usend.at[zl_], urecv.at[j], u_s.at[j], u_r.at[j], z_peer(1, j))

    def t_copy(j):
        return remote(tsend, trecv.at[j], t_s.at[j], t_r.at[j], z_peer(1, j))

    for k in range(3):
        b_second(k)
    slot_forward()
    a_second(0, (1, 2))
    b_second(3)

    @pl.loop(1, 4)
    def _(j):
        y_msg(j).wait_recv()

    tails = jnp.sum(mrecv[:, pl.ds(64, 16), :].astype(f32), axis=0)
    tsend[...] = stack([tails[0:1] + tails[1:2], tails[2:3] + tails[3:4]], 0)[:8]

    @pl.loop(1, 4)
    def _(j):
        t_copy(j).start()

    def z_copy(kk, j):
        zl_ = lax.rem(zl + j, 4)
        i = kk * 4 + j
        return remote(zsend.at[kk, zl_], zrecv.at[kk, j], z_s.at[i], z_r.at[i], z_peer(kk, j))

    z_all = [(0, 0), (0, 1), (0, 2), (0, 3), (1, 1), (1, 2), (1, 3)]

    def last_stage(kk):
        ta = aown[kk, pl.ds(pl.multiple_of(y * 128, 128), 128), :]
        tb = bown[4 * kk + 3]
        for j in range(1, 4):
            a2_copy(kk, j).wait_recv()
            ta = ta + a2recv[kk, j].astype(f32)
            b2_copy(4 * kk + j - 1).wait_recv()
            tb = tb + b2recv[4 * kk + j - 1].astype(f32)
        for zl_, piece in enumerate((ta[:64], ta[64:], tb[:64], tb[64:])):
            tt32[kk, zl_] = piece
            zsend[kk, zl_] = piece.astype(bf16)
        for j in range(kk, 4):
            z_copy(kk, j).start()

    slot_recv()
    own_cols = ds(chip * 128, 128)
    grad_cols = lax.dot_general(
        sgf[...], wu[own_cols, :], (((1,), (1,)), ((), ())), preferred_element_type=f32
    )
    enc[...] = (grad_cols * eslope[:, own_cols]).astype(bf16)

    def enc_copy(j):
        return remote(enc, erecv.at[y], e_s.at[j], e_r.at[j], y_peer(j))

    @pl.loop(1, 4)
    def _(j):
        enc_copy(j).start()

    erecv[y] = enc[...]

    user_part = jnp.dot(
        user_cols, mrecv[:, pl.ds(0, 64), :].reshape(256, 128), preferred_element_type=f32
    ).reshape(4, 64, 128)
    u32[...] = user_part
    usend[...] = user_part.astype(bf16)

    @pl.loop(1, 4)
    def _(j):
        u_copy(j).start()

    b_second(4)
    for k in (5, 6, 7):
        b_second(k, (1, 2, 3))
    a_second(1, (0, 1, 2))

    totals = tsend[...]
    for j in range(1, 4):
        t_copy(j).wait_recv()
        totals = totals + trecv[j]
    frecv[d] = totals
    f_start, f_forward, f_recv, f_send = gather(lambda i: frecv.at[i], f_s, f_r)
    f_start()

    last_stage(0)

    @pl.loop(1, 4)
    def _(j):
        enc_copy(j).wait_recv()

    enc_part = jnp.dot(hist_cols, erecv[...].reshape(256, 128), preferred_element_type=f32)
    enc_part = jnp.where(c == 0, enc_part[:, :64], enc_part[:, 64:]).reshape(4, 2, 32, 64)
    enc_part = jnp.concatenate([enc_part[:, 0], enc_part[:, 1]], axis=2)
    n32[...] = enc_part
    nsend[...] = enc_part.astype(bf16)

    def n_copy(j):
        zl_ = lax.rem(zl + j, 4)
        return remote(nsend.at[zl_], nrecv.at[j], n_s.at[j], n_r.at[j], z_peer(1, j))

    @pl.loop(1, 4)
    def _(j):
        n_copy(j).start()

    last_stage(1)

    sixteen = ds(lax.div(d, 4) * 16, 16)
    grad_rows = lax.dot_general(
        sgf[sixteen, :], wu[...], (((1,), (1,)), ((), ())), preferred_element_type=f32
    )
    enc_rows = (grad_rows * eslope[sixteen, :]).astype(bf16)
    hist_all = grad_rows + lax.dot_general(
        enc_rows, we[...], (((1,), (1,)), ((), ())), preferred_element_type=f32
    )
    place = lax.rem(d, 4)
    hist_grad = hist_all[:4]
    for i in range(1, 4):
        hist_grad = jnp.where(place == i, hist_all[4 * i : 4 * i + 4], hist_grad)
    for k in range(8):
        out_ref[pl.ds(224 + 8 * k, 4), :] = hist_grad[:, 128 * k : 128 * k + 128]

    f_forward()

    user_out = u32[zl]
    for j in range(1, 4):
        u_copy(j).wait_recv()
        user_out = user_out + urecv[j].astype(f32)
    out_ref[pl.ds(64, 64), :] = user_out

    cand = tt32[1, zl]
    for kk, j in z_all:
        z_copy(kk, j).wait_recv()
        cand = cand + zrecv[kk, j].astype(f32)
    out_ref[pl.ds(0, 64), :] = cand

    enc_out = n32[zl]
    for j in range(1, 4):
        n_copy(j).wait_recv()
        enc_out = enc_out + nrecv[j].astype(f32)
    out_ref[pl.ds(128, 32), pl.ds(0, 64)] = enc_out[:, :64]
    out_ref[pl.ds(160, 32), pl.ds(0, 64)] = enc_out[:, 64:]

    f_recv()

    final = frecv[...]
    out_ref[pl.ds(192, 16), :] = final[:, 1, :]
    out_ref[pl.ds(208, 16), :] = final[:, 0, :]

    hist_send()
    slot_send()
    f_send()

    @pl.loop(0, 8)
    def _(k):
        core_copy(k).wait_send()
        s_copy(k, 1).wait_send()

        @pl.when(k != 7)
        def _():
            s_copy(k, 0).wait_send()

        b_copy(k, 1).wait_send()
        b_copy(k, 3).wait_send()

        @pl.when(k < 5)
        def _():
            for i in range(2):
                b_half(k, i).wait_send()

        @pl.when(k >= 5)
        def _():
            b_copy(k, 2).wait_send()

        @pl.when(lax.rem(k, 4) != 3)
        def _():
            b2_copy(k).wait_send()

        @pl.when((lax.rem(k, 4) != 3) & (k > 0))
        def _():
            a_copy(k).wait_send()

    @pl.loop(1, 4)
    def _(j):
        group_copy(j).wait_send()
        group_on(j).wait_send()
        y_msg(j).wait_send()
        enc_copy(j).wait_send()
        u_copy(j).wait_send()
        t_copy(j).wait_send()
        n_copy(j).wait_send()
        for kk in range(2):
            a2_copy(kk, j).wait_send()

    for i in range(2):
        a_half(i).wait_send()

    for kk, j in z_all:
        z_copy(kk, j).wait_send()


def unpack(packed, cg_ref, ug_ref, eg_ref, sc_ref, bi_ref, hg_ref):
    cg_ref[...] = packed[pl.ds(0, 64), :]
    ug_ref[...] = packed[pl.ds(64, 64), :]
    eg_ref[...] = packed[pl.ds(128, 64), pl.ds(0, 64)]
    sc_ref[...] = packed[pl.ds(192, 16), :]
    bi_ref[...] = packed[pl.ds(208, 16), :]
    for k in range(8):
        hg_ref[0, :, pl.ds(128 * k, 128)] = packed[pl.ds(224 + 8 * k, 4), :]


def local(
    history,
    candidates,
    score_grad,
    req_counts,
    owner_slot,
    encoder_weight,
    user_weight,
    cand_weight,
    hidden_bias,
    scorer_weight,
):
    vmem = pl.BlockSpec(memory_space=pltpu.VMEM)
    hbm = pl.BlockSpec(memory_space=pl.ANY)
    V = pltpu.VMEM
    dma = lambda n: pltpu.SemaphoreType.DMA((n,))
    scratch = [
        V((1, 4, D), bf16),
        V((8, 128), f32),
        V((1, SLOTS), jnp.int32),
        V((1, SLOTS), jnp.int32),
        V((1, H), f32),
        V((1, H), f32),
        V((C, D), bf16),
        V((C, 128), bf16),
        V((D, C), bf16),
        V((SLOTS, C), bf16),
        V((D, D), bf16),
        V((D, H), bf16),
        V((D, H), bf16),
        V((C, 128), f32),
        V((8, C, 256), f32),
        V((3, C, 256), bf16),
        V((3, C, 256), bf16),
        V((2, C, 256), bf16),
        V((128, 256), bf16),
        V((32, 128), f32),
        V((16, 32, 128), bf16),
        V((512, 128), f32),
        V((64, D), f32),
        V((128, D), bf16),
        V((64, D), f32),
        V((4, 128, 256), bf16),
        V((2, D, 128), f32),
        V((8, D, 128), bf16),
        V((8, D, 128), bf16),
        V((4, D, 128), f32),
        V((2, 256, 128), bf16),
        V((5, 2, 64, 128), bf16),
        V((8, 512, 128), bf16),
        V((8, 512, 128), bf16),
        V((2, 512, 128), f32),
        V((8, 4, 128, 128), bf16),
        V((8, 4, 128, 128), bf16),
        V((8, 128, 128), f32),
        V((8, 2, 80, 128), bf16),
        V((8, 2, 80, 128), bf16),
        V((80, 128), f32),
        V((80, 128), bf16),
        V((64, H), bf16),
        V((4, 80, 128), bf16),
        V((2, 4, 128, 128), bf16),
        V((2, 4, 128, 128), bf16),
        V((8, 128, 128), bf16),
        V((8, 128, 128), bf16),
        V((2, 4, 64, 128), f32),
        V((2, 4, 64, 128), bf16),
        V((2, 4, 64, 128), bf16),
        V((64, 128), bf16),
        V((4, 64, 128), bf16),
        V((4, 64, 128), f32),
        V((4, 64, 128), bf16),
        V((4, 64, 128), bf16),
        V((4, 32, 128), f32),
        V((4, 32, 128), bf16),
        V((4, 32, 128), bf16),
        V((8, 128), f32),
        V((4, 8, 128), f32),
        V((16, 8, 128), f32),
        dma(10),
    ]
    for n in (16, 4, 4, 2, 10, 8, 8, 32, 16, 16, 4, 8, 8, 8, 4, 4, 4, 4, 16):
        scratch += [dma(n), dma(n)]
    packed = pl.pallas_call(
        kernel,
        out_shape=jax.ShapeDtypeStruct((PACKED, 128), f32),
        in_specs=[hbm] * 10,
        out_specs=vmem,
        scratch_shapes=scratch,
        compiler_params=pltpu.CompilerParams(
            collective_id=0, has_side_effects=True, vmem_limit_bytes=56 * 2**20
        ),
        name="ranking_backward",
    )(
        history,
        score_grad.reshape(8, 128),
        req_counts,
        owner_slot,
        hidden_bias.reshape(1, H),
        scorer_weight.reshape(1, H),
        candidates,
        encoder_weight,
        user_weight,
        cand_weight,
    )
    cg, ug, eg, sc, bi, hg = pl.pallas_call(
        unpack,
        out_shape=(
            jax.ShapeDtypeStruct((64, 128), f32),
            jax.ShapeDtypeStruct((64, 128), f32),
            jax.ShapeDtypeStruct((64, 64), f32),
            jax.ShapeDtypeStruct((16, 128), f32),
            jax.ShapeDtypeStruct((16, 128), f32),
            jax.ShapeDtypeStruct((1, 4, D), f32),
        ),
        in_specs=[vmem],
        out_specs=(vmem,) * 6,
        name="unpack",
    )(packed)
    return (cg, ug, eg, sc.reshape(H), bi.reshape(H), hg)


def solution(mesh):
    in_specs = (
        P("grp", "dev", None),
        P("grp", "dev", None),
        P("grp", "dev"),
        P("grp", None),
        P("grp", None),
        P(),
        P(),
        P(),
        P(),
        P(),
    )
    out_specs = (P("grp", "dev"), P("grp", "dev"), P("grp", "dev"), P(), P(), P("grp", "dev", None))
    return jax.shard_map(local, mesh=mesh, in_specs=in_specs, out_specs=out_specs, check_vma=False)
```
